1024 devices in a mesh: space: 32 (over y, z_lo, core), band: 32 (over z_hi, x).
Axes of the slice: x: 8, y: 8, z: 8 (z_hi: 4, z_lo: 2; z = z_hi * 2 + z_lo), core: 2. Of those that a mesh axis runs over, the one named last changes fastest.
Arguments:
- orbitals: float32 [512, 64, 24, 128], P('band', 'space'), may hold values from -6 to 6
- potential: float32 [64, 24, 128], P('space'), may hold values from 0 to 2
- rotation: float32 [512, 512], P(None, 'band'), may hold values from -0.25 to 0.25
Outputs:
- gram: float32 [512, 512], P('band', 'space')
- projected: float32 [512, 512], P('band', 'space')
- rotated: float32 [512, 64, 24, 128], P('band', 'space')
The draws below stay inside these ranges and needn't reach their ends.
All inputs are finite; a program needn't handle non-finite values.
Results may differ from the reference program's by a relative error of at most 0.004.
Values may be sent and summed in bfloat16 or wider, within the bound.
A program may use at most 32 MiB of HBM per device.

```python
import jax
import jax.numpy as jnp
from jax import lax

ORB = 512
NY = 24
NZ = 128
DEGREE = 8
NX = 64


def shard_levels(key, shape, pieces, low, top_value):
    def one(position, blocks):
        draws = jax.random.uniform(jax.random.fold_in(jax.random.fold_in(key, 6), position), (blocks,), jnp.float32, low / len(pieces), top_value / len(pieces))
        return jnp.repeat(jnp.exp(draws), shape[position] // blocks).reshape((-1,) + (1,) * (len(shape) - position - 1))

    loudness = one(*pieces[0])
    for cut in pieces[1:]:
        loudness = loudness * one(*cut)
    return loudness


def noise(stream_key, extent, width, bound, cuts=(), kind=jnp.bfloat16):
    drawn = jax.random.normal(stream_key, extent, jnp.float32) * width
    if len(cuts) > 0:
        drawn = shard_levels(stream_key, extent, cuts, -0.22, 0.18) * drawn
    return jnp.clip(drawn, min=-bound, max=bound).astype(kind)


def setup_inputs(seed: int = 0) -> dict:
    streams_of = jax.random.split(jax.random.key(seed), 4)
    orbitals = noise(streams_of[0], (ORB, NX, NY, NZ), 1.0, 6.0, ((0, 32), (1, 32)), jnp.float32)
    potential = jnp.clip(2.0 * jax.random.uniform(streams_of[1], (NX, NY, NZ), jnp.float32) ** shard_levels(streams_of[1], (NX, NY, NZ), ((0, 32),), -0.2, 0.2), 0.0, 2.0)
    rotation = noise(streams_of[2], (ORB, ORB), ORB ** -0.5, 0.25, ((1, 32),), jnp.float32)
    return dict(orbitals=orbitals, potential=potential, rotation=rotation)


FILTER_LOW = 2.0
FILTER_HIGH = 8.0
LOWER_EDGE = 0.0


def hamilton(values, potential):
    padded = jnp.pad(values, ((0, 0), (1, 1), (1, 1), (1, 1)))
    neighbours = padded[:, 2:, 1:-1, 1:-1] + padded[:, :-2, 1:-1, 1:-1]
    neighbours = neighbours + padded[:, 1:-1, 2:, 1:-1] + padded[:, 1:-1, :-2, 1:-1]
    neighbours = neighbours + padded[:, 1:-1, 1:-1, 2:] + padded[:, 1:-1, 1:-1, :-2]
    return -0.5 * (neighbours - 6.0 * values) + potential[None] * values


def chebyshev(start_values, potential):
    half_width = (FILTER_HIGH - FILTER_LOW) / 2.0
    centre = (FILTER_HIGH + FILTER_LOW) / 2.0
    first = half_width / (LOWER_EDGE - centre)
    ratio_now = first
    previous = start_values
    current = (first / half_width) * (hamilton(start_values, potential) - centre * start_values)
    for degree_step in range(DEGREE - 1):
        ratio_next = 1.0 / (2.0 / first - ratio_now)
        upcoming = (2.0 * ratio_next / half_width) * (hamilton(current, potential) - centre * current) - (ratio_now * ratio_next) * previous
        previous = current
        current = upcoming
        ratio_now = ratio_next
    return current


def reference(orbitals, potential, rotation):
    filtered = chebyshev(orbitals, potential)
    filtered_b = filtered.astype(jnp.bfloat16)
    applied_b = hamilton(filtered_b.astype(jnp.float32), potential).astype(jnp.bfloat16)
    flat_f = filtered_b.reshape(ORB, -1)
    flat_h = applied_b.reshape(ORB, -1)
    gram = lax.dot_general(flat_f, flat_f, (((1,), (1,)), ((), ())), preferred_element_type=jnp.float32)
    projected = lax.dot_general(flat_h, flat_f, (((1,), (1,)), ((), ())), preferred_element_type=jnp.float32)
    rotation_b = rotation.astype(jnp.bfloat16)
    rotated = lax.dot_general(rotation_b, flat_f, (((0,), (0,)), ((), ())), preferred_element_type=jnp.float32)
    return gram, projected, rotated.reshape(orbitals.shape)
```

```python
import functools

import jax
import jax.numpy as jnp
from jax import lax
from jax.experimental import pallas as pl
from jax.experimental.pallas import tpu as pltpu
from jax.sharding import PartitionSpec as P

DEGREE = 8
FILTER_LOW = 2.0
FILTER_HIGH = 8.0
LOWER_EDGE = 0.0
MESH = pl.DeviceIdType.MESH
VMEM = pltpu.VMEM
F32 = jnp.float32
BF16 = jnp.bfloat16

ZH = 4
Z = 8
NY = 24
NZ = 128
CHUNKS = 3
ROWS = NY // CHUNKS


def steps():
    half_width = (FILTER_HIGH - FILTER_LOW) / 2.0
    centre = (FILTER_HIGH + FILTER_LOW) / 2.0
    first = half_width / (LOWER_EDGE - centre)
    ratio = first
    out = [(first / half_width, 0.0)]
    for _ in range(DEGREE - 1):
        ratio_next = 1.0 / (2.0 / first - ratio)
        out.append((2.0 * ratio_next / half_width, ratio * ratio_next))
        ratio = ratio_next
    return centre, out


def position(n_x):
    bi, si = lax.axis_index("band"), lax.axis_index("space")
    zh, x = bi // n_x, lax.rem(bi, n_x)
    y, q = si // 4, lax.rem(si, 4)
    zl, c = q // 2, lax.rem(q, 2)
    return zh, x, y, q, zl, c


def send(src, dst, send_sem, recv_sem, band, space):
    copy = pltpu.make_async_remote_copy(
        src_ref=src,
        dst_ref=dst,
        send_sem=send_sem,
        recv_sem=recv_sem,
        device_id={"band": band, "space": space},
        device_id_type=MESH,
    )
    return copy


def side_sum(v):
    n = v.shape[0]
    row = lax.broadcasted_iota(jnp.int32, (1, NY, 1), 1)
    lane = lax.broadcasted_iota(jnp.int32, (1, NZ), 1)
    above = jnp.where(row == 0, 0.0, pltpu.roll(v, 1, 1))
    below = jnp.where(row == NY - 1, 0.0, pltpu.roll(v, NY - 1, 1))
    flat = v.reshape(n * NY, NZ)
    left = jnp.where(lane == 0, 0.0, pltpu.roll(flat, 1, 1))
    right = jnp.where(lane == NZ - 1, 0.0, pltpu.roll(flat, NZ - 1, 1))
    return (above + below) + (left + right).reshape(n, NY, NZ)


def filter_kernel(
    n_x, n_y, orb, pot, rt, f1, h1, rt_all,
    ext, work, pv, edge, fb, hb, fr, hr,
    a_send, a_recv, b_send, b_recv, v_send, v_recv, d_send, d_recv,
    f_send, f_recv, h_send, h_recv, r_send, r_recv,
):
    zh, x, y, q, zl, c = position(n_x)
    z = zh * 2 + zl
    me_b, me_s = zh * n_x + x, y * 4 + q
    low, high = y > 0, y < n_y - 1

    @pl.when(y == 0)
    def _():
        for o in range(4):
            ext[o, 0:8] = jnp.zeros((8, NY, NZ), F32)
        pv[0] = jnp.zeros((2, 2, 2, NY, NZ), F32)
        edge[0] = jnp.zeros((4, NY, NZ), F32)

    @pl.when(y == n_y - 1)
    def _():
        for o in range(4):
            ext[o, 16:24] = jnp.zeros((8, NY, NZ), F32)
        pv[2] = jnp.zeros((2, 2, 2, NY, NZ), F32)
        edge[1] = jnp.zeros((4, NY, NZ), F32)

    def along_z(d):
        other = lax.rem(z + d, Z)
        return other, (other // 2) * n_x + x, y * 4 + lax.rem(other, 2) * 2 + c

    barrier = pltpu.get_barrier_semaphore()

    def greet(band, space):
        pl.semaphore_signal(
            barrier, inc=1, device_id={"band": band, "space": space}, device_id_type=MESH
        )

    for d in range(1, Z):
        _, band, space = along_z(d)
        greet(band, space)
    greet(me_b, y * 4 + zl * 2 + (1 - c))
    greet(me_b, y * 4 + (1 - zl) * 2 + (1 - c))

    @pl.when(low)
    def _():
        greet(me_b, me_s - 4)

    @pl.when(high)
    def _():
        greet(me_b, me_s + 4)

    pl.semaphore_wait(barrier, Z + 1 + low.astype(jnp.int32) + high.astype(jnp.int32))

    mate = y * 4 + (1 - zl) * 2 + c
    core = y * 4 + zl * 2 + (1 - c)
    v_mate = send(pot, pv.at[1, zl, c], v_send.at[0], v_recv.at[0], me_b, mate)
    v_mate.start()

    def a_copy(o, d):
        to = lax.rem(q + d, 4)
        return send(
            orb.at[4 * to + o], ext.at[o, pl.ds(8 + 2 * q, 2)],
            a_send.at[o, d - 1], a_recv.at[o, d - 1], me_b, y * 4 + to,
        )

    for o in range(4):
        for d in (2, 1, 3):
            a_copy(o, d).start()

    def r_copy(d):
        to = lax.rem(zh + d, ZH)
        return send(
            rt, rt_all.at[pl.ds(pl.multiple_of(16 * zh, 16), 16)],
            r_send.at[d - 1], r_recv.at[d - 1], to * n_x + x, me_s,
        )

    pv[1, zl, c] = pot[...]
    for o in range(4):
        ext[o, pl.ds(8 + 2 * q, 2)] = orb[4 * q + o]
    rt_all[pl.ds(pl.multiple_of(16 * zh, 16), 16)] = rt[...]

    v_mate.wait_recv()
    v_up = send(pv.at[1, :, c], pv.at[0, :, c], v_send.at[1], v_recv.at[1], me_b, me_s + 4)
    v_down = send(pv.at[1, :, c], pv.at[2, :, c], v_send.at[2], v_recv.at[2], me_b, me_s - 4)

    @pl.when(high)
    def _():
        v_up.start()

    @pl.when(low)
    def _():
        v_down.start()

    def up(o):
        return send(
            ext.at[o, 8:16], ext.at[o, 0:8], b_send.at[o, 0], b_recv.at[o, 0], me_b, me_s + 4
        )

    def down(o):
        return send(
            ext.at[o, 8:16], ext.at[o, 16:24], b_send.at[o, 1], b_recv.at[o, 1], me_b, me_s - 4
        )

    for o in range(4):
        for d in (2, 1, 3):
            a_copy(o, d).wait_recv()

        @pl.when(high)
        def _():
            up(o).start()

        @pl.when(low)
        def _():
            down(o).start()

    for d in range(1, ZH):
        r_copy(d).start()

    @pl.when(low)
    def _():
        v_up.wait_recv()

    @pl.when(high)
    def _():
        v_down.wait_recv()

    v_core = send(pv.at[:, :, c], pv.at[:, :, c], v_send.at[3], v_recv.at[3], me_b, core)
    v_core.start()
    send(
        pv.at[:, :, 1 - c], pv.at[:, :, 1 - c], v_send.at[3], v_recv.at[3], me_b, core
    ).wait_recv()

    centre, coefficients = steps()
    flag_low = jnp.where(low, 1.0, 0.0).astype(F32)
    flag_high = jnp.where(high, 1.0, 0.0).astype(F32)

    def potential(p):
        return pv[p // 8, lax.rem(p, 8) // 4, lax.rem(p, 4) // 2, lax.rem(p, 2)]

    def apply(src, s0, dst, d0, first_plane, count, scale, back, shift, clip):
        def body(i, carry):
            p = first_plane + 2 * i
            v = src[pl.ds(s0, 2), pl.ds(p - 1, 4)]
            if back != 0.0:
                old = dst[pl.ds(d0, 2), pl.ds(p, 2)]
            for k in range(2):
                now = v[:, k + 1]
                near = side_sum(now) + (v[:, k] + v[:, k + 2])
                level = (potential(p + k) + shift) * scale
                new = near * (-0.5 * scale) + level[None] * now
                if back != 0.0:
                    new = new - back * old[:, k]
                if clip:
                    here = p + k
                    flag = jnp.where(here < 8, flag_low, jnp.where(here >= 16, flag_high, 1.0))
                    new = new * flag
                dst[pl.ds(d0, 2), p + k] = new
            return carry

        lax.fori_loop(0, count // 2, body, 0)

    def f_copy(pair, d):
        other, band, space = along_z(d)
        return send(
            fb.at[pair, other], fr.at[z, pair],
            f_send.at[pair, d - 1], f_recv.at[pair, d - 1], band, space,
        )

    def h_copy(pair, d):
        other, band, space = along_z(d)
        return send(
            hb.at[pair, other], hr.at[z, pair],
            h_send.at[pair, d - 1], h_recv.at[pair, d - 1], band, space,
        )

    far = (4, 3, 5, 2, 6, 1, 7)

    def edge_up(pair):
        return send(
            ext.at[pl.ds(2 * pair, 2), 15], edge.at[0, pl.ds(2 * pair, 2)],
            d_send.at[pair, 0], d_recv.at[pair, 0], me_b, me_s + 4,
        )

    def edge_down(pair):
        return send(
            ext.at[pl.ds(2 * pair, 2), 8], edge.at[1, pl.ds(2 * pair, 2)],
            d_send.at[pair, 1], d_recv.at[pair, 1], me_b, me_s - 4,
        )

    for pair in range(2):
        for o in (2 * pair, 2 * pair + 1):

            @pl.when(low)
            def _():
                up(o).wait_recv()
                down(o).wait_send()

            @pl.when(high)
            def _():
                down(o).wait_recv()
                up(o).wait_send()

        for t, (scale, back) in enumerate(coefficients, 1):
            if t % 2 == 1:
                apply(ext, 2 * pair, work, 0, t, 24 - 2 * t, scale, back, 3.0 - centre, True)
            else:
                apply(work, 0, ext, 2 * pair, t, 24 - 2 * t, scale, back, 3.0 - centre, True)

        def rounded(p, carry):
            value = ext[pl.ds(2 * pair, 2), 8 + p].reshape(2 * NY, NZ).astype(BF16)
            fb[pair, p] = value
            ext[pl.ds(2 * pair, 2), 8 + p] = value.astype(F32).reshape(2, NY, NZ)
            return carry

        lax.fori_loop(0, 8, rounded, 0)

        @pl.when(high)
        def _():
            edge_up(pair).start()

        @pl.when(low)
        def _():
            edge_down(pair).start()

        for d in far:
            f_copy(pair, d).start()
        fr[z, pair] = fb[pair, z]

    for pair in range(2):

        @pl.when(low)
        def _():
            edge_up(pair).wait_recv()

        @pl.when(high)
        def _():
            edge_down(pair).wait_recv()

        ext[pl.ds(2 * pair, 2), 7] = edge[0, pl.ds(2 * pair, 2)]
        ext[pl.ds(2 * pair, 2), 16] = edge[1, pl.ds(2 * pair, 2)]
        apply(ext, 2 * pair, work, 0, 8, 8, 1.0, 0.0, 3.0, False)

        def stored(p, carry):
            hb[pair, p] = work[:, 8 + p].reshape(2 * NY, NZ).astype(BF16)
            return carry

        lax.fori_loop(0, 8, stored, 0)
        for d in far:
            h_copy(pair, d).start()
        hr[z, pair] = hb[pair, z]

    def turned(src, dst):
        value = src[...].reshape(Z * 4 * NY, NZ).astype(F32).reshape(Z * 4, NY, NZ)
        dst[...] = jnp.swapaxes(value, 0, 1).reshape(NY * Z * 4, NZ).astype(BF16).reshape(
            NY, Z * 4, NZ
        )

    for pair in range(2):
        for d in range(1, Z):
            f_copy(pair, d).wait_recv()
    turned(fr, f1)
    for pair in range(2):
        for d in range(1, Z):
            h_copy(pair, d).wait_recv()
    turned(hr, h1)

    for d in range(1, ZH):
        r_copy(d).wait()
    for o in range(4):
        for d in range(1, 4):
            a_copy(o, d).wait_send()
    v_mate.wait_send()
    v_core.wait_send()
    for pair in range(2):
        for d in range(1, Z):
            f_copy(pair, d).wait_send()
            h_copy(pair, d).wait_send()

    @pl.when(high)
    def _():
        v_up.wait_send()
        for pair in range(2):
            edge_up(pair).wait_send()

    @pl.when(low)
    def _():
        v_down.wait_send()
        for pair in range(2):
            edge_down(pair).wait_send()


def filtered_blocks(n_x, n_y, orbitals, potential, rt):
    dma = pltpu.SemaphoreType.DMA
    return pl.pallas_call(
        functools.partial(filter_kernel, n_x, n_y),
        out_shape=(
            jax.ShapeDtypeStruct((NY, 4 * Z, NZ), BF16),
            jax.ShapeDtypeStruct((NY, 4 * Z, NZ), BF16),
            jax.ShapeDtypeStruct((16 * ZH, rt.shape[1]), BF16),
        ),
        in_specs=[pl.BlockSpec(memory_space=VMEM)] * 3,
        out_specs=[pl.BlockSpec(memory_space=VMEM)] * 3,
        scratch_shapes=[
            VMEM((4, 24, NY, NZ), F32),
            VMEM((2, 24, NY, NZ), F32),
            VMEM((3, 2, 2, 2, NY, NZ), F32),
            VMEM((2, 4, NY, NZ), F32),
            VMEM((2, Z, 2 * NY, NZ), BF16),
            VMEM((2, Z, 2 * NY, NZ), BF16),
            VMEM((Z, 2, 2 * NY, NZ), BF16),
            VMEM((Z, 2, 2 * NY, NZ), BF16),
            dma((4, 3)), dma((4, 3)), dma((4, 2)), dma((4, 2)), dma((4,)), dma((4,)),
            dma((2, 2)), dma((2, 2)), dma((2, Z - 1)), dma((2, Z - 1)),
            dma((2, Z - 1)), dma((2, Z - 1)), dma((ZH - 1,)), dma((ZH - 1,)),
        ],
        compiler_params=pltpu.CompilerParams(
            collective_id=0, has_side_effects=True, vmem_limit_bytes=40 * 2**20
        ),
    )(orbitals, potential, rt)


def hops(n_x, chunk):
    right, left = n_x // 2, (n_x - 1) // 2
    return (left, right) if chunk % 2 == 1 else (right, left)


def product_kernel(
    n_x, n_y, f1, h1, rt_all, rotated, blocks,
    got, acc, rows, turned, part, summed, last,
    right_send, right_recv, left_send, left_recv, core_send, core_recv,
    back_send, back_recv, y_send, y_recv, z_send, z_recv, own_sem,
):
    zh, x, y, q, zl, c = position(n_x)
    z = zh * 2 + zl
    me_b, me_s = zh * n_x + x, y * 4 + q
    right_b = zh * n_x + lax.rem(x + 1, n_x)
    left_b = zh * n_x + lax.rem(x + n_x - 1, n_x)
    core = y * 4 + zl * 2 + (1 - c)

    barrier = pltpu.get_barrier_semaphore()

    def greet(band, space):
        pl.semaphore_signal(
            barrier, inc=1, device_id={"band": band, "space": space}, device_id_type=MESH
        )

    def along(e):
        other = lax.rem(z * 2 + c + e, 2 * Z)
        oz, oc = other // 2, lax.rem(other, 2)
        return oz, oc, (oz // 2) * n_x + x, y * 4 + lax.rem(oz, 2) * 2 + oc

    for e in range(1, 2 * Z):
        _, _, band, space = along(e)
        greet(band, space)
    for d in range(1, n_y):
        greet(me_b, lax.rem(y + d, n_y) * 4 + q)
    greet(right_b, me_s)
    greet(left_b, me_s)
    pl.semaphore_wait(barrier, 2 * Z - 1 + n_y - 1 + 2)

    def block(cls, owner, chunk):
        return got.at[cls, owner, pl.ds(chunk * ROWS, ROWS)]

    def go_right(hop, chunk):
        owner = lax.rem(x - hop + n_x, n_x)
        src = f1.at[pl.ds(chunk * ROWS, ROWS)] if hop == 0 else block(c, owner, chunk)
        return send(
            src, block(c, owner, chunk),
            right_send.at[hop, chunk], right_recv.at[hop, chunk], right_b, me_s,
        )

    def go_left(hop, chunk):
        owner = lax.rem(x + hop, n_x)
        src = f1.at[pl.ds(chunk * ROWS, ROWS)] if hop == 0 else block(c, owner, chunk)
        return send(
            src, block(c, owner, chunk),
            left_send.at[hop, chunk], left_recv.at[hop, chunk], left_b, me_s,
        )

    def go_core(slot, chunk):
        owner = lax.rem(x - slot + n_x, n_x)
        src = f1.at[pl.ds(chunk * ROWS, ROWS)] if slot == 0 else block(c, owner, chunk)
        return send(
            src, block(c, owner, chunk),
            core_send.at[slot, chunk], core_recv.at[slot, chunk], me_b, core,
        )

    for chunk in range(CHUNKS):
        n_right, n_left = hops(n_x, chunk)
        if n_right > 0:
            go_right(0, chunk).start()
        if n_left > 0:
            go_left(0, chunk).start()
    for chunk in range(CHUNKS):
        go_core(0, chunk).start()
    own = pltpu.make_async_copy(f1, got.at[c, x], own_sem)
    own.start()
    acc[...] = jnp.zeros_like(acc)
    own.wait()

    def chunk_products(chunk):
        zero = jnp.zeros((64, NZ), BF16)

        def body(k, carry):
            r = chunk * ROWS + k
            ours = jnp.concatenate([f1[r], h1[r]], axis=0)
            factor = jnp.concatenate(
                [
                    jnp.concatenate([ours, zero], axis=0),
                    jnp.concatenate([zero, ours], axis=0),
                ],
                axis=1,
            )
            zero_class = got[0, :, r].reshape(n_x * 32, NZ)
            one_class = got[1, :, r].reshape(n_x * 32, NZ)
            both = jnp.concatenate([zero_class, one_class], axis=1)
            acc[...] += lax.dot_general(
                both, factor, (((1,), (1,)), ((), ())), preferred_element_type=F32
            ).reshape(n_x, 32, NZ)
            every = jnp.concatenate([zero_class, one_class], axis=0)
            rows[k] = jnp.dot(
                rt_all[pl.ds(pl.multiple_of(32 * c, 32), 32)],
                every,
                preferred_element_type=F32,
            )
            return carry

        lax.fori_loop(0, ROWS, body, 0)
        turned[chunk] = jnp.swapaxes(rows[...], 0, 1).reshape(2, 16, ROWS, NZ)

    home_q = z // 2
    home_s = y * 4 + home_q

    def give_back(m, chunk):
        return send(
            turned.at[chunk, m],
            rotated.at[:, lax.rem(z, 2), pl.ds(chunk * ROWS, ROWS)],
            back_send.at[m, chunk], back_recv.at[lax.rem(z, 2), chunk],
            (2 * c + m) * n_x + x, home_s,
        )

    def keep(m, chunk):
        return pltpu.make_async_copy(
            turned.at[chunk, m],
            rotated.at[:, lax.rem(z, 2), pl.ds(chunk * ROWS, ROWS)],
            back_send.at[m, chunk],
        )

    def is_self(m):
        return (home_q == q) & (2 * c + m == zh)

    def come_back(plane, chunk):
        return send(
            turned.at[chunk, 0],
            rotated.at[:, plane, pl.ds(chunk * ROWS, ROWS)],
            back_send.at[0, chunk], back_recv.at[plane, chunk], me_b, core,
        )

    top = max(n_x // 2, 1)
    for hop in range(1, top + 1):
        for chunk in range(CHUNKS):
            n_right, n_left = hops(n_x, chunk)
            if hop <= n_right:
                go_right(hop - 1, chunk).wait_recv()
                if hop < n_right:
                    go_right(hop, chunk).start()
                go_core(hop, chunk).start()
            if hop <= n_left:
                go_left(hop - 1, chunk).wait_recv()
                if hop < n_left:
                    go_left(hop, chunk).start()
                go_core(n_x - hop, chunk).start()

    for chunk in range(CHUNKS):
        for slot in range(n_x):
            go_core(slot, chunk).wait_recv()
        chunk_products(chunk)
        for m in range(2):

            @pl.when(is_self(m))
            def _():
                keep(m, chunk).start()

            @pl.when(jnp.logical_not(is_self(m)))
            def _():
                give_back(m, chunk).start()

    def y_copy(d):
        to = lax.rem(y + d, n_y)
        first = 4 * to
        return send(
            acc.at[
                pl.ds(lax.rem(first, n_x), 4),
                pl.ds(pl.multiple_of(first // n_x * 8, 8), 8),
            ],
            part.at[y], y_send.at[d - 1], y_recv.at[d - 1], me_b, to * 4 + q,
        )

    for d in range(1, n_y):
        y_copy(d).start()
    mine = 4 * y
    part[y] = acc[
        pl.ds(lax.rem(mine, n_x), 4), pl.ds(pl.multiple_of(mine // n_x * 8, 8), 8)
    ]
    for d in range(1, n_y):
        y_copy(d).wait_recv()
    total = part[0]
    for k in range(1, n_y):
        total = total + part[k]
    summed[...] = total

    def z_copy(e):
        oz, oc, band, space = along(e)
        return send(
            summed.at[lax.rem(oz, 2) * 2 + oc], last.at[c, z],
            z_send.at[e - 1], z_recv.at[e - 1], band, space,
        )

    for e in range(1, 2 * Z):
        z_copy(e).start()
    last[c, z] = summed[q]
    for e in range(1, 2 * Z):
        z_copy(e).wait_recv()
    for cls in range(2):
        value = last[cls, 0]
        for k in range(1, Z):
            value = value + last[cls, k]
        blocks[cls] = value

    for plane in range(2):
        from_me = (2 * q + plane == z) & (c == zh // 2)
        for chunk in range(CHUNKS):

            @pl.when(jnp.logical_not(from_me))
            def _():
                come_back(plane, chunk).wait_recv()

    for m in range(2):

        @pl.when(is_self(m))
        def _():
            for chunk in range(CHUNKS):
                keep(m, chunk).wait()

        @pl.when(jnp.logical_not(is_self(m)))
        def _():
            for chunk in range(CHUNKS):
                give_back(m, chunk).wait_send()

    for chunk in range(CHUNKS):
        n_right, n_left = hops(n_x, chunk)
        for hop in range(n_right):
            go_right(hop, chunk).wait_send()
        for hop in range(n_left):
            go_left(hop, chunk).wait_send()
        for slot in range(n_x):
            go_core(slot, chunk).wait_send()
    for d in range(1, n_y):
        y_copy(d).wait_send()
    for e in range(1, 2 * Z):
        z_copy(e).wait_send()


def products(n_x, n_y, f1, h1, rt_all):
    dma = pltpu.SemaphoreType.DMA
    top = max(n_x // 2, 1)
    return pl.pallas_call(
        functools.partial(product_kernel, n_x, n_y),
        out_shape=(
            jax.ShapeDtypeStruct((16, 2, NY, NZ), F32),
            jax.ShapeDtypeStruct((2, 8, NZ), F32),
        ),
        in_specs=[pl.BlockSpec(memory_space=VMEM)] * 3,
        out_specs=[pl.BlockSpec(memory_space=VMEM)] * 2,
        scratch_shapes=[
            VMEM((2, n_x, NY, 32, NZ), BF16),
            VMEM((n_x, 32, NZ), F32),
            VMEM((ROWS, 32, NZ), F32),
            VMEM((CHUNKS, 2, 16, ROWS, NZ), F32),
            VMEM((n_y, 4, 8, NZ), F32),
            VMEM((4, 8, NZ), F32),
            VMEM((2, Z, 8, NZ), F32),
            dma((top, CHUNKS)), dma((top, CHUNKS)), dma((top, CHUNKS)), dma((top, CHUNKS)),
            dma((n_x, CHUNKS)), dma((n_x, CHUNKS)), dma((2, CHUNKS)), dma((2, CHUNKS)),
            dma((max(n_y - 1, 1),)), dma((max(n_y - 1, 1),)),
            dma((2 * Z - 1,)), dma((2 * Z - 1,)), dma(()),
        ],
        compiler_params=pltpu.CompilerParams(
            collective_id=1, has_side_effects=True, vmem_limit_bytes=40 * 2**20
        ),
    )(f1, h1, rt_all)


def shards(orbitals, potential, rotation):
    n_x = lax.axis_size("band") // ZH
    n_y = lax.axis_size("space") // 4
    cols = rotation.shape[1]
    rt = rotation.astype(BF16).reshape(ZH, n_x, 2, 2, 4, cols)
    rt = rt.transpose(5, 3, 1, 0, 2, 4).reshape(cols, -1)
    f1, h1, rt_all = filtered_blocks(n_x, n_y, orbitals, potential, rt)
    rotated, blocks = products(n_x, n_y, f1, h1, rt_all)
    blocks = blocks.reshape(2, 2, 4, 2, 2, ZH, 2, 4)
    blocks = lax.dynamic_index_in_dim(blocks, lax.axis_index("band") // n_x, 5, keepdims=False)
    blocks = blocks.transpose(4, 5, 0, 6, 1, 3, 2).reshape(2, 16, 16)
    return (blocks[0], blocks[1], rotated)


def solution(mesh):
    placed = (P("band", "space", None, None), P("space", None, None), P(None, "band"))
    return jax.shard_map(
        shards,
        mesh=mesh,
        in_specs=placed,
        out_specs=(P("band", "space"), P("band", "space"), P("band", "space", None, None)),
        check_vma=False,
    )
```

```python
import jax
import jax.numpy as jnp
from jax import lax
from jax.experimental import pallas as pl
from jax.experimental.pallas import tpu as pltpu
from jax.sharding import PartitionSpec as P

DEGREE = 8
FILTER_LOW = 2.0
FILTER_HIGH = 8.0
LOWER_EDGE = 0.0
MESH = pl.DeviceIdType.MESH
VMEM = pltpu.VMEM
F32 = jnp.float32
BF16 = jnp.bfloat16

ZH = 4
Z = 8
NY = 24
NZ = 128
PAD = 8
TALL = NY + 2 * PAD
DATA = slice(PAD, PAD + NY)
ROWS = 8
PIECES = ((0, 0, NY), (1, 0, ROWS), (1, ROWS, ROWS), (1, 2 * ROWS, ROWS))
CHUNKS = NY // ROWS


def steps():
    half_width = (FILTER_HIGH - FILTER_LOW) / 2.0
    centre = (FILTER_HIGH + FILTER_LOW) / 2.0
    first = half_width / (LOWER_EDGE - centre)
    ratio = first
    out = [(first / half_width, 0.0)]
    for _ in range(DEGREE - 1):
        ratio_next = 1.0 / (2.0 / first - ratio)
        out.append((2.0 * ratio_next / half_width, ratio * ratio_next))
        ratio = ratio_next
    return centre, out


def hops(n_x, pair):
    right, left = n_x // 2, (n_x - 1) // 2
    return (left, right) if pair == 1 else (right, left)


def send(src, dst, send_sem, recv_sem, band, space):
    return pltpu.make_async_remote_copy(
        src_ref=src,
        dst_ref=dst,
        send_sem=send_sem,
        recv_sem=recv_sem,
        device_id={"band": band, "space": space},
        device_id_type=MESH,
    )


def whole_kernel(
    n_x, n_y, orb, pot, rotation_in, gram, projected, rotated,
    rotation, own_sem, ext, work, pv, edge, rt_all, fb, hb, fr, hr, h_own,
    got, acc, acc_sent, rot, rows, back_out, back_in, part, summed, last,
    a_send, a_recv, b_send, b_recv, v_send, v_recv, d_send, d_recv,
    f_send, f_recv, h_send, h_recv, r_send, r_recv,
    right_send, right_recv, left_send, left_recv, core_send, core_recv,
    back_send, back_recv, y_send, y_recv, z_send, z_recv,
):
    bi, si = lax.axis_index("band"), lax.axis_index("space")
    zh, x = bi // n_x, lax.rem(bi, n_x)
    y, q = si // 4, lax.rem(si, 4)
    zl, c = q // 2, lax.rem(q, 2)
    z = zh * 2 + zl
    low, high = y > 0, y < n_y - 1
    right_b = zh * n_x + lax.rem(x + 1, n_x)
    left_b = zh * n_x + lax.rem(x + n_x - 1, n_x)
    mate = y * 4 + (1 - zl) * 2 + c
    core = y * 4 + zl * 2 + (1 - c)

    def along(e):
        other = lax.rem(z * 2 + c + e, 2 * Z)
        oz, oc = other // 2, lax.rem(other, 2)
        return oz, oc, (oz // 2) * n_x + x, y * 4 + lax.rem(oz, 2) * 2 + oc

    def along_z(d):
        other = lax.rem(z + d, Z)
        return other, (other // 2) * n_x + x, y * 4 + lax.rem(other, 2) * 2 + c

    barrier = pltpu.get_barrier_semaphore()

    def greet(band, space):
        pl.semaphore_signal(
            barrier, inc=1, device_id={"band": band, "space": space}, device_id_type=MESH
        )

    for e in range(1, 2 * Z):
        _, _, band, space = along(e)
        greet(band, space)
    for d in range(1, n_y):
        greet(bi, lax.rem(y + d, n_y) * 4 + q)
    greet(right_b, si)
    greet(left_b, si)

    blank = jnp.zeros((PAD, NZ), F32)

    def clear(p, carry):
        for o in range(4):
            ext[o, p, 0:PAD] = blank
            ext[o, p, PAD + NY : TALL] = blank
        for o in range(2):
            work[o, p, 0:PAD] = blank
            work[o, p, PAD + NY : TALL] = blank
        return carry

    lax.fori_loop(0, 24, clear, 0)

    def empty(first, slab, side):
        def body(p, carry):
            for o in range(4):
                ext[o, first + p, DATA] = jnp.zeros((NY, NZ), F32)
            return carry

        lax.fori_loop(0, 8, body, 0)
        pv[slab] = jnp.zeros((2, 2, 2, NY, NZ), F32)
        edge[side] = jnp.zeros((4, NY, NZ), F32)

    @pl.when(y == 0)
    def _():
        empty(0, 0, 0)

    @pl.when(y == n_y - 1)
    def _():
        empty(16, 2, 1)

    pl.semaphore_wait(barrier, 2 * Z - 1 + n_y - 1 + 2)

    v_mate = send(pot, pv.at[1, zl, c], v_send.at[0], v_recv.at[0], bi, mate)
    v_mate.start()

    def partner(d):
        return (1 - zl if d >= 2 else zl) * 2 + (1 - c if d % 2 else c)

    def pair_of(p):
        return slice(2 * p, 2 * p + 2)

    def a_copy(p, d):
        to = partner(d)
        return send(
            orb.at[pl.ds(4 * to + 2 * p, 2)], ext.at[pair_of(p), pl.ds(8 + 2 * q, 2), DATA],
            a_send.at[p, d - 1], a_recv.at[p, d - 1], bi, y * 4 + to,
        )

    def a_wait(p, d):
        of = partner(d)
        send(
            orb.at[pl.ds(4 * q + 2 * p, 2)], ext.at[pair_of(p), pl.ds(8 + 2 * of, 2), DATA],
            a_send.at[p, d - 1], a_recv.at[p, d - 1], bi, y * 4 + of,
        ).wait_recv()

    def own_copy(p):
        return pltpu.make_async_copy(
            orb.at[pl.ds(4 * q + 2 * p, 2)], ext.at[pair_of(p), pl.ds(8 + 2 * q, 2), DATA],
            own_sem.at[p],
        )

    def b_copy(p, d, side):
        of = partner(d)
        here = ext.at[pair_of(p), pl.ds(8 + 2 * of, 2), DATA]
        if d == 0:
            here = orb.at[pl.ds(4 * q + 2 * p, 2)]
        return send(
            here, ext.at[pair_of(p), pl.ds(16 * side + 2 * of, 2), DATA],
            b_send.at[p, d, side], b_recv.at[p, d, side], bi, si + 4 - 8 * side,
        )

    def pass_on(p, d):
        @pl.when(high)
        def _():
            b_copy(p, d, 0).start()

        @pl.when(low)
        def _():
            b_copy(p, d, 1).start()

    for p in range(2):
        for d in (2, 1, 3):
            a_copy(p, d).start()
        if p == 0:
            pass_on(0, 0)
    load_pot = pltpu.make_async_copy(pot, pv.at[1, zl, c], own_sem.at[2])
    load_pot.start()
    load_rotation = pltpu.make_async_copy(rotation_in, rotation, own_sem.at[3])
    load_rotation.start()
    for p in range(2):
        own_copy(p).start()

    v_up = send(pv.at[1, :, c], pv.at[0, :, c], v_send.at[1], v_recv.at[1], bi, si + 4)
    v_down = send(pv.at[1, :, c], pv.at[2, :, c], v_send.at[2], v_recv.at[2], bi, si - 4)

    a_wait(0, 1)
    pass_on(0, 1)
    load_pot.wait()
    v_mate.wait_recv()

    @pl.when(high)
    def _():
        v_up.start()

    @pl.when(low)
    def _():
        v_down.start()

    a_wait(0, 2)
    pass_on(0, 2)
    a_wait(0, 3)
    pass_on(0, 3)
    pass_on(1, 0)
    for d in (1, 2, 3):
        a_wait(1, d)
        pass_on(1, d)
    load_rotation.wait()
    for p in range(2):
        own_copy(p).wait()

    count = rotation.shape[1]
    i = lax.broadcasted_iota(jnp.int32, (count, count), 0)
    k = lax.broadcasted_iota(jnp.int32, (count, count), 1)
    half = n_x * 16
    source = (
        16 * (((k // 4) % 4) * n_x + (k // 16) % n_x)
        + 8 * ((k // 2) % 2)
        + 4 * ((k // half) % 2)
        + 2 * (k // (2 * half))
        + k % 2
    )
    order = jnp.where(i == source, 1.0, 0.0).astype(BF16)
    my_rt = pl.ds(pl.multiple_of(16 * zh, 16), 16)
    rt_all[my_rt] = lax.dot_general(
        rotation[...].astype(BF16), order, (((1,), (0,)), ((), ())), preferred_element_type=F32
    ).astype(BF16)

    def r_copy(d):
        to = lax.rem(zh + d, ZH)
        return send(
            rt_all.at[my_rt], rt_all.at[my_rt],
            r_send.at[d - 1], r_recv.at[d - 1], to * n_x + x, si,
        )

    def r_wait(d):
        of = lax.rem(zh + ZH - d, ZH)
        theirs = rt_all.at[pl.ds(pl.multiple_of(16 * of, 16), 16)]
        send(theirs, theirs, r_send.at[d - 1], r_recv.at[d - 1], of * n_x + x, si).wait_recv()

    for d in range(1, ZH):
        r_copy(d).start()

    @pl.when(low)
    def _():
        v_up.wait_recv()

    @pl.when(high)
    def _():
        v_down.wait_recv()

    v_core = send(pv.at[:, :, c], pv.at[:, :, c], v_send.at[3], v_recv.at[3], bi, core)
    v_core.start()
    send(
        pv.at[:, :, 1 - c], pv.at[:, :, 1 - c], v_send.at[3], v_recv.at[3], bi, core
    ).wait_recv()

    centre, coefficients = steps()
    lane = lax.broadcasted_iota(jnp.int32, (1, NZ), 1)

    def potential(p):
        return pv[p // 8, lax.rem(p, 8) // 4, lax.rem(p, 4) // 2, lax.rem(p, 2)]

    def planes(src, s0, dst, d0, p, width, scale, back, shift):
        old = dst[pl.ds(d0, 2), pl.ds(p, width), DATA] if back != 0.0 else None
        mid = src[pl.ds(s0, 2), pl.ds(p - 1, width + 2), DATA]
        above = src[pl.ds(s0, 2), pl.ds(p, width), PAD - 1 : PAD + NY - 1]
        below = src[pl.ds(s0, 2), pl.ds(p, width), PAD + 1 : PAD + NY + 1]
        for k in range(width):
            now = mid[:, k + 1]
            flat = now.reshape(2 * NY, NZ)
            left = jnp.where(lane == 0, 0.0, pltpu.roll(flat, 1, 1))
            right = jnp.where(lane == NZ - 1, 0.0, pltpu.roll(flat, NZ - 1, 1))
            near = (left + right).reshape(2, NY, NZ)
            near = near + ((above[:, k] + below[:, k]) + (mid[:, k] + mid[:, k + 2]))
            level = (potential(p + k) + shift) * scale
            new = near * (-0.5 * scale) + level[None] * now
            if back != 0.0:
                new = new - back * old[:, k]
            dst[pl.ds(d0, 2), p + k, DATA] = new

    def apply(src, s0, dst, d0, first, count, scale, back, shift):
        def body(i, carry):
            planes(src, s0, dst, d0, first + 4 * i, 4, scale, back, shift)
            return carry

        lax.fori_loop(0, count // 4, body, 0)
        if count % 4:
            planes(src, s0, dst, d0, first + count - 2, 2, scale, back, shift)

    def f_copy(pair, d):
        other, band, space = along_z(d)
        return send(
            fb.at[pair, other], fr.at[z, pair],
            f_send.at[pair, d - 1], f_recv.at[pair, d - 1], band, space,
        )

    def h_copy(pair, d):
        other, band, space = along_z(d)
        return send(
            hb.at[pair, other], hr.at[z, pair],
            h_send.at[pair, d - 1], h_recv.at[pair, d - 1], band, space,
        )

    far = (4, 3, 5, 2, 6, 1, 7)

    def edge_up(pair):
        return send(
            ext.at[pl.ds(2 * pair, 2), 15, DATA], edge.at[0, pl.ds(2 * pair, 2)],
            d_send.at[pair, 0], d_recv.at[pair, 0], bi, si + 4,
        )

    def edge_down(pair):
        return send(
            ext.at[pl.ds(2 * pair, 2), 8, DATA], edge.at[1, pl.ds(2 * pair, 2)],
            d_send.at[pair, 1], d_recv.at[pair, 1], bi, si - 4,
        )

    def filtered(pair):
        for d in range(4):

            @pl.when(low)
            def _():
                b_copy(pair, d, 0).wait_recv()
                b_copy(pair, d, 1).wait_send()

            @pl.when(high)
            def _():
                b_copy(pair, d, 1).wait_recv()
                b_copy(pair, d, 0).wait_send()

        for t, (scale, back) in enumerate(coefficients, 1):
            src, s0, dst, d0 = (ext, 2 * pair, work, 0) if t % 2 else (work, 0, ext, 2 * pair)
            apply(src, s0, dst, d0, t, 24 - 2 * t, scale, back, 3.0 - centre)
            if t < DEGREE:

                @pl.when(y == 0)
                def _():
                    dst[pl.ds(d0, 2), 7, DATA] = jnp.zeros((2, NY, NZ), F32)

                @pl.when(y == n_y - 1)
                def _():
                    dst[pl.ds(d0, 2), 16, DATA] = jnp.zeros((2, NY, NZ), F32)

        def rounded(p, carry):
            value = ext[pl.ds(2 * pair, 2), 8 + p, DATA].reshape(2 * NY, NZ).astype(BF16)
            fb[pair, p] = value
            ext[pl.ds(2 * pair, 2), 8 + p, DATA] = value.astype(F32).reshape(2, NY, NZ)
            return carry

        lax.fori_loop(0, 8, rounded, 0)
        for d in far:
            f_copy(pair, d).start()
        fr[z, pair] = fb[pair, z]

        @pl.when(high)
        def _():
            edge_up(pair).start()

        @pl.when(low)
        def _():
            edge_down(pair).start()

    def turn(src, pair):
        value = src[:, pair].reshape(Z * 2 * NY, NZ).astype(F32).reshape(Z * 2, NY, NZ)
        value = jnp.swapaxes(value, 0, 1).reshape(NY * Z * 2, NZ).astype(BF16)
        return value.reshape(NY, Z * 2, NZ)

    def block(cls, owner, piece):
        pair, first, size = PIECES[piece]
        return got.at[cls, owner, pair, pl.ds(first, size)]

    def go_right(hop, piece):
        owner = lax.rem(x - hop + n_x, n_x)
        return send(
            block(c, owner, piece), block(c, owner, piece),
            right_send.at[hop, piece], right_recv.at[hop, piece], right_b, si,
        )

    def from_left(hop, piece):
        owner = lax.rem(x - hop - 1 + n_x, n_x)
        return send(
            block(c, owner, piece), block(c, owner, piece),
            right_send.at[hop, piece], right_recv.at[hop, piece], right_b, si,
        )

    def go_left(hop, piece):
        owner = lax.rem(x + hop, n_x)
        return send(
            block(c, owner, piece), block(c, owner, piece),
            left_send.at[hop, piece], left_recv.at[hop, piece], left_b, si,
        )

    def from_right(hop, piece):
        owner = lax.rem(x + hop + 1, n_x)
        return send(
            block(c, owner, piece), block(c, owner, piece),
            left_send.at[hop, piece], left_recv.at[hop, piece], left_b, si,
        )

    def go_core(slot, piece):
        owner = lax.rem(x - slot + n_x, n_x)
        return send(
            block(c, owner, piece), block(c, owner, piece),
            core_send.at[slot, piece], core_recv.at[slot, piece], bi, core,
        )

    def from_core(slot, piece):
        owner = lax.rem(x - slot + n_x, n_x)
        return send(
            block(1 - c, owner, piece), block(1 - c, owner, piece),
            core_send.at[slot, piece], core_recv.at[slot, piece], bi, core,
        )

    def launch(pair):
        for d in range(1, Z):
            f_copy(pair, d).wait_recv()
        got[c, x, pair] = turn(fr, pair)
        n_right, n_left = hops(n_x, pair)
        mine = [k for k in range(len(PIECES)) if PIECES[k][0] == pair]
        for piece in mine:
            if n_right > 0:
                go_right(0, piece).start()
            if n_left > 0:
                go_left(0, piece).start()
        for piece in mine:
            go_core(0, piece).start()

    def serve(hop, piece):
        n_right, n_left = hops(n_x, PIECES[piece][0])
        if hop <= n_right:
            from_left(hop - 1, piece).wait_recv()
            if hop < n_right:
                go_right(hop, piece).start()
            go_core(hop, piece).start()
        if hop <= n_left:
            from_right(hop - 1, piece).wait_recv()
            if hop < n_left:
                go_left(hop, piece).start()
            go_core(n_x - hop, piece).start()

    def applied(pair):
        @pl.when(low)
        def _():
            edge_up(pair).wait_recv()

        @pl.when(high)
        def _():
            edge_down(pair).wait_recv()

        ext[pl.ds(2 * pair, 2), 7, DATA] = edge[0, pl.ds(2 * pair, 2)]
        ext[pl.ds(2 * pair, 2), 16, DATA] = edge[1, pl.ds(2 * pair, 2)]
        apply(ext, 2 * pair, work, 0, 8, 8, 1.0, 0.0, 3.0)

        def stored(p, carry):
            hb[pair, p] = work[:, 8 + p, DATA].reshape(2 * NY, NZ).astype(BF16)
            return carry

        lax.fori_loop(0, 8, stored, 0)
        for d in far:
            h_copy(pair, d).start()
        hr[z, pair] = hb[pair, z]

    def take_applied(pair):
        for d in range(1, Z):
            h_copy(pair, d).wait_recv()
        h_own[pair] = turn(hr, pair)

    def take_core(piece):
        for slot in range(n_x):
            from_core(slot, piece).wait_recv()

    zero = jnp.zeros((4 * 16, NZ), BF16)

    def correlate(piece):
        pair, first, size = PIECES[piece]

        def body(g, carry):
            total = None
            for k in range(ROWS):
                r = first + g * ROWS + k
                ours = jnp.concatenate(
                    [got[c, x, 0, r], got[c, x, 1, r], h_own[0, r], h_own[1, r]], axis=0
                )
                factor = jnp.concatenate(
                    [
                        jnp.concatenate([ours, zero], axis=0),
                        jnp.concatenate([zero, ours], axis=0),
                    ],
                    axis=1,
                )
                both = jnp.concatenate(
                    [got[cls, :, pair, r].reshape(n_x * 16, NZ) for cls in range(2)], axis=1
                )
                value = lax.dot_general(
                    both, factor, (((1,), (1,)), ((), ())), preferred_element_type=F32
                )
                total = value if total is None else total + value
            acc[pair] += total.reshape(n_x, 16, NZ)
            return carry

        lax.fori_loop(0, size // ROWS, body, 0)

    my_rows = pl.ds(pl.multiple_of(32 * c, 32), 32)

    def rotate(piece):
        pair, first, size = PIECES[piece]

        ours = rt_all[my_rows, pair * 2 * half : (pair + 1) * 2 * half]

        def body(g, carry):
            for k in range(ROWS):
                r = first + g * ROWS + k
                every = got[:, :, pair, r].reshape(2 * n_x * 16, NZ)
                value = jnp.dot(ours, every, preferred_element_type=F32)
                if pair == 0:
                    rot[r] = value
                else:
                    rows[k] = rot[r] + value
            return carry

        lax.fori_loop(0, size // ROWS, body, 0)

    home_q = z // 2

    def is_self(m):
        return (home_q == q) & (2 * c + m == zh)

    def give_back(m, chunk):
        return send(
            back_out.at[chunk, m], back_in.at[lax.rem(z, 2), chunk],
            back_send.at[m, chunk], back_recv.at[lax.rem(z, 2), chunk],
            (2 * c + m) * n_x + x, y * 4 + home_q,
        )

    def come_back(plane, chunk):
        return send(
            back_out.at[chunk, 0], back_in.at[plane, chunk],
            back_send.at[0, chunk], back_recv.at[plane, chunk], bi, core,
        )

    def return_rows(chunk):
        value = jnp.swapaxes(rows[...], 0, 1).reshape(2, 16 * ROWS, NZ).astype(BF16)
        back_out[chunk] = value
        for m in range(2):

            @pl.when(is_self(m))
            def _():
                back_in[lax.rem(z, 2), chunk] = back_out[chunk, m]

            @pl.when(jnp.logical_not(is_self(m)))
            def _():
                give_back(m, chunk).start()

    acc[...] = jnp.zeros_like(acc)
    pieces = len(PIECES)
    filtered(0)
    launch(0)
    filtered(1)
    later = range(1, pieces)

    def serve_later(hop):
        for piece in later:
            serve(hop, piece)

    serve(1, 0)
    applied(0)
    serve(2, 0)
    launch(1)
    applied(1)
    serve(3, 0)
    serve_later(1)
    take_applied(0)
    serve(4, 0)
    serve_later(2)
    take_applied(1)
    for d in range(1, ZH):
        r_wait(d)
    take_core(0)
    rotate(0)
    serve_later(3)
    correlate(0)
    serve_later(4)
    for piece in range(1, pieces):
        take_core(piece)
        if piece == pieces - 1:
            break
        rotate(piece)
        return_rows(piece - 1)
        correlate(piece)
    correlate(pieces - 1)

    for pair in range(2):
        for k in range(ZH):
            acc_sent[:, 8 * k + 4 * pair : 8 * k + 4 * pair + 4] = acc[pair, :, 4 * k : 4 * k + 4]

    def columns_of(to):
        first = 4 * to
        return (
            pl.ds(lax.rem(first, n_x), 4),
            pl.ds(pl.multiple_of(first // n_x * 8, 8), 8),
        )

    def y_copy(d):
        to = lax.rem(y + d, n_y)
        return send(
            acc_sent.at[columns_of(to)], part.at[y],
            y_send.at[d - 1], y_recv.at[d - 1], bi, to * 4 + q,
        )

    for d in range(1, n_y):
        y_copy(d).start()
    part[y] = acc_sent[columns_of(y)]
    rotate(pieces - 1)
    return_rows(CHUNKS - 1)
    for d in range(1, n_y):
        y_copy(d).wait_recv()
    total = part[0]
    for k in range(1, n_y):
        total = total + part[k]
    summed[...] = total

    def z_copy(e):
        oz, oc, band, space = along(e)
        return send(
            summed.at[lax.rem(oz, 2) * 2 + oc], last.at[c, z],
            z_send.at[e - 1], z_recv.at[e - 1], band, space,
        )

    for e in range(1, 2 * Z):
        z_copy(e).start()
    last[c, z] = summed[q]

    for chunk in range(CHUNKS):
        for plane in range(2):
            from_me = (2 * q + plane == z) & (c == zh // 2)

            @pl.when(jnp.logical_not(from_me))
            def _():
                come_back(plane, chunk).wait_recv()

            rotated[:, plane, chunk * ROWS : (chunk + 1) * ROWS] = (
                back_in[plane, chunk].astype(F32).reshape(16, ROWS, NZ)
            )

    for e in range(1, 2 * Z):
        z_copy(e).wait_recv()
    n = lax.broadcasted_iota(jnp.int32, (64, NZ), 0)
    l = lax.broadcasted_iota(jnp.int32, (64, NZ), 1)
    lane_of = (
        64 * ((n // 16) % 2) + 32 * (n // 32)
        + 16 * ((n // 2) % 2) + 4 * zh + 2 * ((n // 8) % 2) + n % 2
    )
    picked = None
    for cls in range(2):
        value = last[cls, 0]
        for k in range(1, Z):
            value = value + last[cls, k]
        select = jnp.where((l == lane_of) & ((n // 4) % 2 == cls), 1.0, 0.0)
        value = lax.dot_general(
            select, value, (((1,), (1,)), ((), ())),
            precision=lax.Precision.HIGHEST, preferred_element_type=F32,
        )
        picked = value if picked is None else picked + value
    r = lax.broadcasted_iota(jnp.int32, (8, 16), 0)
    i = lax.broadcasted_iota(jnp.int32, (8, 16), 1)
    for side, out in enumerate((gram, projected)):
        value = None
        for cls in range(2):
            select = jnp.where(
                i == 8 * ((r // 2) % 2) + 4 * cls + 2 * (r // 4) + r % 2, 1.0, 0.0
            )
            first = 32 * side + 16 * cls
            term = jnp.dot(
                picked[first : first + 16], select,
                precision=lax.Precision.HIGHEST, preferred_element_type=F32,
            )
            value = term if value is None else value + term
        out[...] = value

    for d in range(1, ZH):
        r_copy(d).wait_send()
    for p in range(2):
        for d in range(1, 4):
            a_copy(p, d).wait_send()
    v_mate.wait_send()
    v_core.wait_send()
    for pair in range(2):
        for d in range(1, Z):
            f_copy(pair, d).wait_send()
            h_copy(pair, d).wait_send()

    @pl.when(high)
    def _():
        v_up.wait_send()
        for pair in range(2):
            edge_up(pair).wait_send()

    @pl.when(low)
    def _():
        v_down.wait_send()
        for pair in range(2):
            edge_down(pair).wait_send()

    for piece in range(pieces):
        n_right, n_left = hops(n_x, PIECES[piece][0])
        for hop in range(n_right):
            go_right(hop, piece).wait_send()
        for hop in range(n_left):
            go_left(hop, piece).wait_send()
        for slot in range(n_x):
            go_core(slot, piece).wait_send()
    for chunk in range(CHUNKS):
        for m in range(2):

            @pl.when(jnp.logical_not(is_self(m)))
            def _():
                give_back(m, chunk).wait_send()

    for d in range(1, n_y):
        y_copy(d).wait_send()
    for e in range(1, 2 * Z):
        z_copy(e).wait_send()


def shards(orbitals, potential, rotation):
    n_x = lax.axis_size("band") // ZH
    n_y = lax.axis_size("space") // 4
    top, pieces = max(n_x // 2, 1), len(PIECES)
    dma = pltpu.SemaphoreType.DMA

    def kernel(*refs):
        whole_kernel(n_x, n_y, *refs)

    return pl.pallas_call(
        kernel,
        out_shape=(
            jax.ShapeDtypeStruct((16, 16), F32),
            jax.ShapeDtypeStruct((16, 16), F32),
            jax.ShapeDtypeStruct(orbitals.shape, F32),
        ),
        in_specs=[pl.BlockSpec(memory_space=pltpu.HBM)] * 3,
        out_specs=[pl.BlockSpec(memory_space=VMEM)] * 3,
        scratch_shapes=[
            VMEM(rotation.shape[::-1], F32), dma((4,)),
            VMEM((4, 24, TALL, NZ), F32),
            VMEM((2, 24, TALL, NZ), F32),
            VMEM((3, 2, 2, 2, NY, NZ), F32),
            VMEM((2, 4, NY, NZ), F32),
            VMEM((16 * ZH, rotation.shape[0]), BF16),
            VMEM((2, Z, 2 * NY, NZ), BF16),
            VMEM((2, Z, 2 * NY, NZ), BF16),
            VMEM((Z, 2, 2 * NY, NZ), BF16),
            VMEM((Z, 2, 2 * NY, NZ), BF16),
            VMEM((2, NY, 2 * Z, NZ), BF16),
            VMEM((2, n_x, 2, NY, 2 * Z, NZ), BF16),
            VMEM((2, n_x, 2 * Z, NZ), F32),
            VMEM((n_x, 4 * Z, NZ), F32),
            VMEM((NY, 32, NZ), F32),
            VMEM((ROWS, 32, NZ), F32),
            VMEM((CHUNKS, 2, 16 * ROWS, NZ), BF16),
            VMEM((2, CHUNKS, 16 * ROWS, NZ), BF16),
            VMEM((n_y, 4, 8, NZ), F32),
            VMEM((4, 8, NZ), F32),
            VMEM((2, Z, 8, NZ), F32),
            dma((2, 3)), dma((2, 3)), dma((2, 4, 2)), dma((2, 4, 2)), dma((4,)), dma((4,)),
            dma((2, 2)), dma((2, 2)), dma((2, Z - 1)), dma((2, Z - 1)),
            dma((2, Z - 1)), dma((2, Z - 1)), dma((ZH - 1,)), dma((ZH - 1,)),
            dma((top, pieces)), dma((top, pieces)), dma((top, pieces)), dma((top, pieces)),
            dma((n_x, pieces)), dma((n_x, pieces)), dma((2, CHUNKS)), dma((2, CHUNKS)),
            dma((n_y - 1,)), dma((n_y - 1,)), dma((2 * Z - 1,)), dma((2 * Z - 1,)),
        ],
        compiler_params=pltpu.CompilerParams(
            collective_id=0, has_side_effects=True, vmem_limit_bytes=60 * 2**20
        ),
    )(orbitals, potential, rotation.T)


def solution(mesh):
    placed = (P("band", "space", None, None), P("space", None, None), P(None, "band"))
    return jax.shard_map(
        shards,
        mesh=mesh,
        in_specs=placed,
        out_specs=(P("band", "space"), P("band", "space"), P("band", "space", None, None)),
        check_vma=False,
    )
```

```python
import jax
import jax.numpy as jnp
from jax import lax
from jax.experimental import pallas as pl
from jax.experimental.pallas import tpu as pltpu
from jax.sharding import PartitionSpec as P

DEGREE = 8
FILTER_LOW = 2.0
FILTER_HIGH = 8.0
LOWER_EDGE = 0.0
MESH = pl.DeviceIdType.MESH
VMEM = pltpu.VMEM
F32 = jnp.float32
BF16 = jnp.bfloat16

ZH = 4
Z = 8
NY = 24
NZ = 128
PAD = 8
TALL = NY + 2 * PAD
DATA = slice(PAD, PAD + NY)
ROWS = 8
CHUNKS = NY // ROWS
PIECES = tuple((pair, ROWS * k, ROWS) for pair in range(2) for k in range(CHUNKS))


def steps():
    half_width = (FILTER_HIGH - FILTER_LOW) / 2.0
    centre = (FILTER_HIGH + FILTER_LOW) / 2.0
    first = half_width / (LOWER_EDGE - centre)
    ratio = first
    out = [(first / half_width, 0.0)]
    for _ in range(DEGREE - 1):
        ratio_next = 1.0 / (2.0 / first - ratio)
        out.append((2.0 * ratio_next / half_width, ratio * ratio_next))
        ratio = ratio_next
    return centre, out


def hops(n_x, pair):
    right, left = n_x // 2, (n_x - 1) // 2
    return (left, right) if pair == 1 else (right, left)


def send(src, dst, send_sem, recv_sem, band, space):
    return pltpu.make_async_remote_copy(
        src_ref=src,
        dst_ref=dst,
        send_sem=send_sem,
        recv_sem=recv_sem,
        device_id={"band": band, "space": space},
        device_id_type=MESH,
    )


def whole_kernel(
    n_x, n_y, orb, pot, rotation_in, gram, projected, rotated,
    rotation, own_sem, ext, work, pv, edge, rt_all, fb, hb, fr, hr, h_own,
    got, acc, acc_sent, rot, rows, back_out, back_in, part, summed, last, sums, done,
    a_send, a_recv, b_send, b_recv, v_send, v_recv, d_send, d_recv,
    f_send, f_recv, h_send, h_recv, r_send, r_recv,
    right_send, right_recv, left_send, left_recv, core_send, core_recv,
    back_send, back_recv, y_send, y_recv, z_send, z_recv,
):
    bi, si = lax.axis_index("band"), lax.axis_index("space")
    zh, x = bi // n_x, lax.rem(bi, n_x)
    y, q = si // 4, lax.rem(si, 4)
    zl, c = q // 2, lax.rem(q, 2)
    z = zh * 2 + zl
    low, high = y > 0, y < n_y - 1
    right_b = zh * n_x + lax.rem(x + 1, n_x)
    left_b = zh * n_x + lax.rem(x + n_x - 1, n_x)
    mate = y * 4 + (1 - zl) * 2 + c
    core = y * 4 + zl * 2 + (1 - c)

    def along(e):
        other = lax.rem(z * 2 + c + e, 2 * Z)
        oz, oc = other // 2, lax.rem(other, 2)
        return oz, oc, (oz // 2) * n_x + x, y * 4 + lax.rem(oz, 2) * 2 + oc

    def along_z(d):
        other = lax.rem(z + d, Z)
        return other, (other // 2) * n_x + x, y * 4 + lax.rem(other, 2) * 2 + c

    barrier = pltpu.get_barrier_semaphore()

    def greet(band, space):
        pl.semaphore_signal(
            barrier, inc=1, device_id={"band": band, "space": space}, device_id_type=MESH
        )

    for e in range(1, 2 * Z):
        _, _, band, space = along(e)
        greet(band, space)
    for d in range(1, n_y):
        greet(bi, lax.rem(y + d, n_y) * 4 + q)
    greet(right_b, si)
    greet(left_b, si)

    blank = jnp.zeros((PAD, NZ), F32)

    def clear(p, carry):
        for o in range(4):
            ext[o, p, 0:PAD] = blank
            ext[o, p, PAD + NY : TALL] = blank
        for o in range(2):
            work[o, p, 0:PAD] = blank
            work[o, p, PAD + NY : TALL] = blank
        return carry

    lax.fori_loop(0, 24, clear, 0)

    def empty(first, slab, side):
        def body(p, carry):
            for o in range(4):
                ext[o, first + p, DATA] = jnp.zeros((NY, NZ), F32)
            return carry

        lax.fori_loop(0, 8, body, 0)
        pv[slab] = jnp.zeros((2, 2, 2, NY, NZ), F32)
        edge[side] = jnp.zeros((4, NY, NZ), F32)

    @pl.when(y == 0)
    def _():
        empty(0, 0, 0)

    @pl.when(y == n_y - 1)
    def _():
        empty(16, 2, 1)

    pl.semaphore_wait(barrier, 2 * Z - 1 + n_y - 1 + 2)

    v_mate = send(pot, pv.at[1, zl, c], v_send.at[0], v_recv.at[0], bi, mate)
    v_mate.start()

    def partner(d):
        return (1 - zl if d >= 2 else zl) * 2 + (1 - c if d % 2 else c)

    def pair_of(p):
        return slice(2 * p, 2 * p + 2)

    def a_copy(p, d):
        to = partner(d)
        return send(
            orb.at[pl.ds(4 * to + 2 * p, 2)], ext.at[pair_of(p), pl.ds(8 + 2 * q, 2), DATA],
            a_send.at[p, d - 1], a_recv.at[p, d - 1], bi, y * 4 + to,
        )

    def a_wait(p, d):
        of = partner(d)
        send(
            orb.at[pl.ds(4 * q + 2 * p, 2)], ext.at[pair_of(p), pl.ds(8 + 2 * of, 2), DATA],
            a_send.at[p, d - 1], a_recv.at[p, d - 1], bi, y * 4 + of,
        ).wait_recv()

    def own_copy(p):
        return pltpu.make_async_copy(
            orb.at[pl.ds(4 * q + 2 * p, 2)], ext.at[pair_of(p), pl.ds(8 + 2 * q, 2), DATA],
            own_sem.at[p],
        )

    def b_copy(p, d, side):
        of = partner(d)
        here = ext.at[pair_of(p), pl.ds(8 + 2 * of, 2), DATA]
        if d == 0:
            here = orb.at[pl.ds(4 * q + 2 * p, 2)]
        return send(
            here, ext.at[pair_of(p), pl.ds(16 * side + 2 * of, 2), DATA],
            b_send.at[p, d, side], b_recv.at[p, d, side], bi, si + 4 - 8 * side,
        )

    def pass_on(p, d):
        @pl.when(high)
        def _():
            b_copy(p, d, 0).start()

        @pl.when(low)
        def _():
            b_copy(p, d, 1).start()

    for p in range(2):
        for d in (2, 1, 3):
            a_copy(p, d).start()
        if p == 0:
            pass_on(0, 0)
    load_pot = pltpu.make_async_copy(pot, pv.at[1, zl, c], own_sem.at[2])
    load_pot.start()
    load_rotation = pltpu.make_async_copy(rotation_in, rotation, own_sem.at[3])
    load_rotation.start()
    for p in range(2):
        own_copy(p).start()

    v_up = send(pv.at[1, :, c], pv.at[0, :, c], v_send.at[1], v_recv.at[1], bi, si + 4)
    v_down = send(pv.at[1, :, c], pv.at[2, :, c], v_send.at[2], v_recv.at[2], bi, si - 4)

    a_wait(0, 1)
    pass_on(0, 1)
    load_pot.wait()
    v_mate.wait_recv()

    @pl.when(high)
    def _():
        v_up.start()

    @pl.when(low)
    def _():
        v_down.start()

    a_wait(0, 2)
    pass_on(0, 2)
    a_wait(0, 3)
    pass_on(0, 3)
    pass_on(1, 0)
    for d in (1, 2, 3):
        a_wait(1, d)
        pass_on(1, d)
    load_rotation.wait()
    for p in range(2):
        own_copy(p).wait()

    count = rotation.shape[1]
    i = lax.broadcasted_iota(jnp.int32, (count, count), 0)
    k = lax.broadcasted_iota(jnp.int32, (count, count), 1)
    half = n_x * 16
    source = (
        16 * (((k // 4) % 4) * n_x + (k // 16) % n_x)
        + 8 * ((k // 2) % 2)
        + 4 * ((k // half) % 2)
        + 2 * (k // (2 * half))
        + k % 2
    )
    order = jnp.where(i == source, 1.0, 0.0).astype(BF16)
    my_rt = pl.ds(pl.multiple_of(16 * zh, 16), 16)
    rt_all[my_rt] = lax.dot_general(
        rotation[...].astype(BF16), order, (((1,), (0,)), ((), ())), preferred_element_type=F32
    ).astype(BF16)

    def r_copy(d):
        to = lax.rem(zh + d, ZH)
        return send(
            rt_all.at[my_rt], rt_all.at[my_rt],
            r_send.at[d - 1], r_recv.at[d - 1], to * n_x + x, si,
        )

    def r_wait(d):
        of = lax.rem(zh + ZH - d, ZH)
        theirs = rt_all.at[pl.ds(pl.multiple_of(16 * of, 16), 16)]
        send(theirs, theirs, r_send.at[d - 1], r_recv.at[d - 1], of * n_x + x, si).wait_recv()

    for d in range(1, ZH):
        r_copy(d).start()

    @pl.when(low)
    def _():
        v_up.wait_recv()

    @pl.when(high)
    def _():
        v_down.wait_recv()

    v_core = send(pv.at[:, :, c], pv.at[:, :, c], v_send.at[3], v_recv.at[3], bi, core)
    v_core.start()
    send(
        pv.at[:, :, 1 - c], pv.at[:, :, 1 - c], v_send.at[3], v_recv.at[3], bi, core
    ).wait_recv()

    centre, coefficients = steps()
    lane = lax.broadcasted_iota(jnp.int32, (1, NZ), 1)

    def potential(p):
        return pv[p // 8, lax.rem(p, 8) // 4, lax.rem(p, 4) // 2, lax.rem(p, 2)]

    def planes(src, s0, dst, d0, p, width, scale, back, shift):
        old = dst[pl.ds(d0, 2), pl.ds(p, width), DATA] if back != 0.0 else None
        mid = src[pl.ds(s0, 2), pl.ds(p - 1, width + 2), DATA]
        above = src[pl.ds(s0, 2), pl.ds(p, width), PAD - 1 : PAD + NY - 1]
        below = src[pl.ds(s0, 2), pl.ds(p, width), PAD + 1 : PAD + NY + 1]
        for k in range(width):
            now = mid[:, k + 1]
            flat = now.reshape(2 * NY, NZ)
            left = jnp.where(lane == 0, 0.0, pltpu.roll(flat, 1, 1))
            right = jnp.where(lane == NZ - 1, 0.0, pltpu.roll(flat, NZ - 1, 1))
            near = (left + right).reshape(2, NY, NZ)
            near = near + ((above[:, k] + below[:, k]) + (mid[:, k] + mid[:, k + 2]))
            level = (potential(p + k) + shift) * scale
            new = near * (-0.5 * scale) + level[None] * now
            if back != 0.0:
                new = new - back * old[:, k]
            dst[pl.ds(d0, 2), p + k, DATA] = new

    def apply(src, s0, dst, d0, first, count, scale, back, shift):
        def body(i, carry):
            planes(src, s0, dst, d0, first + 4 * i, 4, scale, back, shift)
            return carry

        lax.fori_loop(0, count // 4, body, 0)
        if count % 4:
            planes(src, s0, dst, d0, first + count - 2, 2, scale, back, shift)

    def f_copy(pair, d):
        other, band, space = along_z(d)
        return send(
            fb.at[pair, other], fr.at[z, pair],
            f_send.at[pair, d - 1], f_recv.at[pair, d - 1], band, space,
        )

    def h_copy(pair, d):
        other, band, space = along_z(d)
        return send(
            hb.at[pair, other], hr.at[z, pair],
            h_send.at[pair, d - 1], h_recv.at[pair, d - 1], band, space,
        )

    far = (4, 3, 5, 2, 6, 1, 7)

    def edge_up(pair):
        return send(
            ext.at[pl.ds(2 * pair, 2), 15, DATA], edge.at[0, pl.ds(2 * pair, 2)],
            d_send.at[pair, 0], d_recv.at[pair, 0], bi, si + 4,
        )

    def edge_down(pair):
        return send(
            ext.at[pl.ds(2 * pair, 2), 8, DATA], edge.at[1, pl.ds(2 * pair, 2)],
            d_send.at[pair, 1], d_recv.at[pair, 1], bi, si - 4,
        )

    def filtered(pair):
        for d in range(4):

            @pl.when(low)
            def _():
                b_copy(pair, d, 0).wait_recv()
                b_copy(pair, d, 1).wait_send()

            @pl.when(high)
            def _():
                b_copy(pair, d, 1).wait_recv()
                b_copy(pair, d, 0).wait_send()

        for t, (scale, back) in enumerate(coefficients, 1):
            src, s0, dst, d0 = (ext, 2 * pair, work, 0) if t % 2 else (work, 0, ext, 2 * pair)
            apply(src, s0, dst, d0, t, 24 - 2 * t, scale, back, 3.0 - centre)
            if t < DEGREE:

                @pl.when(y == 0)
                def _():
                    dst[pl.ds(d0, 2), 7, DATA] = jnp.zeros((2, NY, NZ), F32)

                @pl.when(y == n_y - 1)
                def _():
                    dst[pl.ds(d0, 2), 16, DATA] = jnp.zeros((2, NY, NZ), F32)

        def rounded(p, carry):
            value = ext[pl.ds(2 * pair, 2), 8 + p, DATA].reshape(2 * NY, NZ).astype(BF16)
            fb[pair, p] = value
            ext[pl.ds(2 * pair, 2), 8 + p, DATA] = value.astype(F32).reshape(2, NY, NZ)
            return carry

        lax.fori_loop(0, 8, rounded, 0)
        for d in far:
            f_copy(pair, d).start()
        fr[z, pair] = fb[pair, z]

        @pl.when(high)
        def _():
            edge_up(pair).start()

        @pl.when(low)
        def _():
            edge_down(pair).start()

    def turn(src, pair):
        value = src[:, pair].reshape(Z * 2 * NY, NZ).astype(F32).reshape(Z * 2, NY, NZ)
        value = jnp.swapaxes(value, 0, 1).reshape(NY * Z * 2, NZ).astype(BF16)
        return value.reshape(NY, Z * 2, NZ)

    def block(cls, owner, piece):
        pair, first, size = PIECES[piece]
        return got.at[cls, owner, pair, pl.ds(first, size)]

    def go_right(hop, piece):
        owner = lax.rem(x - hop + n_x, n_x)
        return send(
            block(c, owner, piece), block(c, owner, piece),
            right_send.at[hop, piece], right_recv.at[hop, piece], right_b, si,
        )

    def from_left(hop, piece):
        owner = lax.rem(x - hop - 1 + n_x, n_x)
        return send(
            block(c, owner, piece), block(c, owner, piece),
            right_send.at[hop, piece], right_recv.at[hop, piece], right_b, si,
        )

    def go_left(hop, piece):
        owner = lax.rem(x + hop, n_x)
        return send(
            block(c, owner, piece), block(c, owner, piece),
            left_send.at[hop, piece], left_recv.at[hop, piece], left_b, si,
        )

    def from_right(hop, piece):
        owner = lax.rem(x + hop + 1, n_x)
        return send(
            block(c, owner, piece), block(c, owner, piece),
            left_send.at[hop, piece], left_recv.at[hop, piece], left_b, si,
        )

    def go_core(slot, piece):
        owner = lax.rem(x - slot + n_x, n_x)
        return send(
            block(c, owner, piece), block(c, owner, piece),
            core_send.at[slot, piece], core_recv.at[slot, piece], bi, core,
        )

    def from_core(slot, piece):
        owner = lax.rem(x - slot + n_x, n_x)
        return send(
            block(1 - c, owner, piece), block(1 - c, owner, piece),
            core_send.at[slot, piece], core_recv.at[slot, piece], bi, core,
        )

    def launch(pair):
        for d in range(1, Z):
            f_copy(pair, d).wait_recv()
        got[c, x, pair] = turn(fr, pair)
        n_right, n_left = hops(n_x, pair)
        mine = [k for k in range(len(PIECES)) if PIECES[k][0] == pair]
        for piece in mine:
            if n_right > 0:
                go_right(0, piece).start()
            if n_left > 0:
                go_left(0, piece).start()
        for piece in mine:
            go_core(0, piece).start()

    def serve(hop, piece):
        n_right, n_left = hops(n_x, PIECES[piece][0])
        if hop <= n_right:
            from_left(hop - 1, piece).wait_recv()
            if hop < n_right:
                go_right(hop, piece).start()
            go_core(hop, piece).start()
        if hop <= n_left:
            from_right(hop - 1, piece).wait_recv()
            if hop < n_left:
                go_left(hop, piece).start()
            go_core(n_x - hop, piece).start()

    def applied(pair):
        @pl.when(low)
        def _():
            edge_up(pair).wait_recv()

        @pl.when(high)
        def _():
            edge_down(pair).wait_recv()

        ext[pl.ds(2 * pair, 2), 7, DATA] = edge[0, pl.ds(2 * pair, 2)]
        ext[pl.ds(2 * pair, 2), 16, DATA] = edge[1, pl.ds(2 * pair, 2)]
        apply(ext, 2 * pair, work, 0, 8, 8, 1.0, 0.0, 3.0)

        def stored(p, carry):
            hb[pair, p] = work[:, 8 + p, DATA].reshape(2 * NY, NZ).astype(BF16)
            return carry

        lax.fori_loop(0, 8, stored, 0)
        for d in far:
            h_copy(pair, d).start()
        hr[z, pair] = hb[pair, z]

    def take_applied(pair):
        for d in range(1, Z):
            h_copy(pair, d).wait_recv()
        h_own[pair] = turn(hr, pair)

    def take_core(piece):
        for slot in range(n_x):
            from_core(slot, piece).wait_recv()

    zero = jnp.zeros((4 * 16, NZ), BF16)

    def correlate(piece):
        pair, first, size = PIECES[piece]

        def body(g, carry):
            total = None
            for k in range(ROWS):
                r = first + g * ROWS + k
                ours = jnp.concatenate(
                    [got[c, x, 0, r], got[c, x, 1, r], h_own[0, r], h_own[1, r]], axis=0
                )
                factor = jnp.concatenate(
                    [
                        jnp.concatenate([ours, zero], axis=0),
                        jnp.concatenate([zero, ours], axis=0),
                    ],
                    axis=1,
                )
                both = jnp.concatenate(
                    [got[cls, :, pair, r].reshape(n_x * 16, NZ) for cls in range(2)], axis=1
                )
                value = lax.dot_general(
                    both, factor, (((1,), (1,)), ((), ())), preferred_element_type=F32
                )
                total = value if total is None else total + value
            acc[pair] += total.reshape(n_x, 16, NZ)
            return carry

        lax.fori_loop(0, size // ROWS, body, 0)

    my_rows = pl.ds(pl.multiple_of(32 * c, 32), 32)

    def rotate(piece):
        pair, first, size = PIECES[piece]

        ours = rt_all[my_rows, pair * 2 * half : (pair + 1) * 2 * half]

        def body(g, carry):
            for k in range(ROWS):
                r = first + g * ROWS + k
                every = got[:, :, pair, r].reshape(2 * n_x * 16, NZ)
                value = jnp.dot(ours, every, preferred_element_type=F32)
                if pair == 0:
                    rot[r] = value
                else:
                    rows[k] = rot[r] + value
            return carry

        lax.fori_loop(0, size // ROWS, body, 0)

    home_q = z // 2

    def is_self(m):
        return (home_q == q) & (2 * c + m == zh)

    def give_back(m, chunk):
        return send(
            back_out.at[chunk, m], back_in.at[lax.rem(z, 2), chunk],
            back_send.at[m, chunk], back_recv.at[lax.rem(z, 2), chunk],
            (2 * c + m) * n_x + x, y * 4 + home_q,
        )

    def come_back(plane, chunk):
        return send(
            back_out.at[chunk, 0], back_in.at[plane, chunk],
            back_send.at[0, chunk], back_recv.at[plane, chunk], bi, core,
        )

    def return_rows(chunk):
        value = jnp.swapaxes(rows[...], 0, 1).reshape(2, 16 * ROWS, NZ).astype(BF16)
        back_out[chunk] = value
        for m in range(2):

            @pl.when(is_self(m))
            def _():
                back_in[lax.rem(z, 2), chunk] = back_out[chunk, m]

            @pl.when(jnp.logical_not(is_self(m)))
            def _():
                give_back(m, chunk).start()

    def y_copy(pair, d):
        to = lax.rem(y + d, n_y)
        return send(
            acc_sent.at[pair, to], part.at[pair, y],
            y_send.at[pair, d - 1], y_recv.at[pair, d - 1], bi, to * 4 + q,
        )

    def y_begin(pair):
        for to in range(n_y):
            for k in range(4):
                zh_i, x_i = (4 * to + k) // n_x, (4 * to + k) % n_x
                acc_sent[pair, to, 4 * k : 4 * k + 4] = acc[pair, x_i, 4 * zh_i : 4 * zh_i + 4]
        for d in sorted(range(1, n_y), key=lambda d: -min(d, n_y - d)):
            y_copy(pair, d).start()
        part[pair, y] = acc_sent[pair, y]

    acc[...] = jnp.zeros_like(acc)
    pieces = len(PIECES)
    filtered(0)
    filtered(1)
    launch(0)

    def serve_pair(hop, pair):
        for piece in range(CHUNKS * pair, CHUNKS * (pair + 1)):
            serve(hop, piece)

    applied(0)
    serve_pair(1, 0)
    launch(1)
    applied(1)
    serve_pair(2, 0)
    serve_pair(1, 1)
    take_applied(0)
    serve_pair(3, 0)
    serve_pair(2, 1)
    take_applied(1)
    for d in range(1, ZH):
        r_wait(d)
    serve_pair(4, 0)
    serve_pair(3, 1)
    for piece in range(CHUNKS):
        take_core(piece)
        rotate(piece)
        correlate(piece)
    serve_pair(4, 1)
    y_begin(0)
    for piece in range(CHUNKS, pieces):
        take_core(piece)
        if piece == pieces - 1:
            break
        rotate(piece)
        return_rows(piece - CHUNKS)
        correlate(piece)
    correlate(pieces - 1)

    y_begin(1)
    rotate(pieces - 1)
    return_rows(CHUNKS - 1)
    for pair in range(2):
        for d in range(1, n_y):
            y_copy(pair, d).wait_recv()
        total = part[pair, 0]
        for k in range(1, n_y):
            total = total + part[pair, k]
        for k in range(4):
            summed[k // 2, k % 2, 4 * pair : 4 * pair + 4] = total[4 * k : 4 * k + 4]

    def z_copy(d):
        oz, band, space = along_z(d)
        return send(
            summed.at[lax.rem(oz, 2)], last.at[z],
            z_send.at[d - 1], z_recv.at[d - 1], band, space,
        )

    for d in far:
        z_copy(d).start()
    last[z] = summed[zl]

    for chunk in range(CHUNKS):
        for plane in range(2):
            from_me = (2 * q + plane == z) & (c == zh // 2)

            @pl.when(jnp.logical_not(from_me))
            def _():
                come_back(plane, chunk).wait_recv()

            rotated[:, plane, chunk * ROWS : (chunk + 1) * ROWS] = (
                back_in[plane, chunk].astype(F32).reshape(16, ROWS, NZ)
            )

    for d in range(1, Z):
        z_copy(d).wait_recv()
    value = last[0]
    for k in range(1, Z):
        value = value + last[k]
    sums[0] = value
    done[c] = sums[0, c]
    trade = send(
        sums.at[0, 1 - c], done.at[c], v_send.at[4], v_recv.at[4], bi, core
    )
    trade.start()
    send(
        sums.at[0, c], done.at[1 - c], v_send.at[4], v_recv.at[4], bi, core
    ).wait_recv()
    n = lax.broadcasted_iota(jnp.int32, (64, NZ), 0)
    l = lax.broadcasted_iota(jnp.int32, (64, NZ), 1)
    lane_of = (
        64 * ((n // 16) % 2) + 32 * (n // 32)
        + 16 * ((n // 2) % 2) + 4 * zh + 2 * ((n // 8) % 2) + n % 2
    )
    picked = None
    for cls in range(2):
        value = done[cls]
        select = jnp.where((l == lane_of) & ((n // 4) % 2 == cls), 1.0, 0.0)
        value = lax.dot_general(
            select, value, (((1,), (1,)), ((), ())),
            precision=lax.Precision.HIGHEST, preferred_element_type=F32,
        )
        picked = value if picked is None else picked + value
    r = lax.broadcasted_iota(jnp.int32, (8, 16), 0)
    i = lax.broadcasted_iota(jnp.int32, (8, 16), 1)
    for side, out in enumerate((gram, projected)):
        value = None
        for cls in range(2):
            select = jnp.where(
                i == 8 * ((r // 2) % 2) + 4 * cls + 2 * (r // 4) + r % 2, 1.0, 0.0
            )
            first = 32 * side + 16 * cls
            term = jnp.dot(
                picked[first : first + 16], select,
                precision=lax.Precision.HIGHEST, preferred_element_type=F32,
            )
            value = term if value is None else value + term
        out[...] = value

    for d in range(1, ZH):
        r_copy(d).wait_send()
    for p in range(2):
        for d in range(1, 4):
            a_copy(p, d).wait_send()
    v_mate.wait_send()
    v_core.wait_send()
    for pair in range(2):
        for d in range(1, Z):
            f_copy(pair, d).wait_send()
            h_copy(pair, d).wait_send()

    @pl.when(high)
    def _():
        v_up.wait_send()
        for pair in range(2):
            edge_up(pair).wait_send()

    @pl.when(low)
    def _():
        v_down.wait_send()
        for pair in range(2):
            edge_down(pair).wait_send()

    for piece in range(pieces):
        n_right, n_left = hops(n_x, PIECES[piece][0])
        for hop in range(n_right):
            go_right(hop, piece).wait_send()
        for hop in range(n_left):
            go_left(hop, piece).wait_send()
        for slot in range(n_x):
            go_core(slot, piece).wait_send()
    for chunk in range(CHUNKS):
        for m in range(2):

            @pl.when(jnp.logical_not(is_self(m)))
            def _():
                give_back(m, chunk).wait_send()

    for pair in range(2):
        for d in range(1, n_y):
            y_copy(pair, d).wait_send()
    for d in range(1, Z):
        z_copy(d).wait_send()
    trade.wait_send()


def shards(orbitals, potential, rotation):
    n_x = lax.axis_size("band") // ZH
    n_y = lax.axis_size("space") // 4
    top, pieces = max(n_x // 2, 1), len(PIECES)
    dma = pltpu.SemaphoreType.DMA

    def kernel(*refs):
        whole_kernel(n_x, n_y, *refs)

    return pl.pallas_call(
        kernel,
        out_shape=(
            jax.ShapeDtypeStruct((16, 16), F32),
            jax.ShapeDtypeStruct((16, 16), F32),
            jax.ShapeDtypeStruct(orbitals.shape, F32),
        ),
        in_specs=[pl.BlockSpec(memory_space=pltpu.HBM)] * 3,
        out_specs=[pl.BlockSpec(memory_space=VMEM)] * 3,
        scratch_shapes=[
            VMEM(rotation.shape[::-1], F32), dma((4,)),
            VMEM((4, 24, TALL, NZ), F32),
            VMEM((2, 24, TALL, NZ), F32),
            VMEM((3, 2, 2, 2, NY, NZ), F32),
            VMEM((2, 4, NY, NZ), F32),
            VMEM((16 * ZH, rotation.shape[0]), BF16),
            VMEM((2, Z, 2 * NY, NZ), BF16),
            VMEM((2, Z, 2 * NY, NZ), BF16),
            VMEM((Z, 2, 2 * NY, NZ), BF16),
            VMEM((Z, 2, 2 * NY, NZ), BF16),
            VMEM((2, NY, 2 * Z, NZ), BF16),
            VMEM((2, n_x, 2, NY, 2 * Z, NZ), BF16),
            VMEM((2, n_x, 2 * Z, NZ), F32),
            VMEM((2, n_y, 16, NZ), F32),
            VMEM((NY, 32, NZ), F32),
            VMEM((ROWS, 32, NZ), F32),
            VMEM((CHUNKS, 2, 16 * ROWS, NZ), BF16),
            VMEM((2, CHUNKS, 16 * ROWS, NZ), BF16),
            VMEM((2, n_y, 16, NZ), F32),
            VMEM((2, 2, 8, NZ), F32),
            VMEM((Z, 2, 8, NZ), F32),
            VMEM((1, 2, 8, NZ), F32),
            VMEM((2, 8, NZ), F32),
            dma((2, 3)), dma((2, 3)), dma((2, 4, 2)), dma((2, 4, 2)), dma((5,)), dma((5,)),
            dma((2, 2)), dma((2, 2)), dma((2, Z - 1)), dma((2, Z - 1)),
            dma((2, Z - 1)), dma((2, Z - 1)), dma((ZH - 1,)), dma((ZH - 1,)),
            dma((top, pieces)), dma((top, pieces)), dma((top, pieces)), dma((top, pieces)),
            dma((n_x, pieces)), dma((n_x, pieces)), dma((2, CHUNKS)), dma((2, CHUNKS)),
            dma((2, n_y - 1)), dma((2, n_y - 1)), dma((Z - 1,)), dma((Z - 1,)),
        ],
        compiler_params=pltpu.CompilerParams(
            collective_id=0, has_side_effects=True, vmem_limit_bytes=60 * 2**20
        ),
    )(orbitals, potential, rotation.T)


def solution(mesh):
    placed = (P("band", "space", None, None), P("space", None, None), P(None, "band"))
    return jax.shard_map(
        shards,
        mesh=mesh,
        in_specs=placed,
        out_specs=(P("band", "space"), P("band", "space"), P("band", "space", None, None)),
        check_vma=False,
    )
```

```python
import jax
import jax.numpy as jnp
from jax import lax
from jax.experimental import pallas as pl
from jax.experimental.pallas import tpu as pltpu
from jax.sharding import PartitionSpec as P

DEGREE = 8
FILTER_LOW = 2.0
FILTER_HIGH = 8.0
LOWER_EDGE = 0.0
MESH = pl.DeviceIdType.MESH
VMEM = pltpu.VMEM
F32 = jnp.float32
BF16 = jnp.bfloat16

ZH = 4
Z = 8
NY = 24
NZ = 128
PAD = 8
TALL = NY + 2 * PAD
DATA = slice(PAD, PAD + NY)
ROWS = 8
CHUNKS = NY // ROWS
PIECES = tuple((pair, ROWS * k, ROWS) for pair in range(2) for k in range(CHUNKS))


def steps():
    half_width = (FILTER_HIGH - FILTER_LOW) / 2.0
    centre = (FILTER_HIGH + FILTER_LOW) / 2.0
    first = half_width / (LOWER_EDGE - centre)
    ratio = first
    out = [(first / half_width, 0.0)]
    for _ in range(DEGREE - 1):
        ratio_next = 1.0 / (2.0 / first - ratio)
        out.append((2.0 * ratio_next / half_width, ratio * ratio_next))
        ratio = ratio_next
    return centre, out


def hops(n_x, pair):
    right, left = n_x // 2, (n_x - 1) // 2
    return (left, right) if pair == 1 else (right, left)


def send(src, dst, send_sem, recv_sem, band, space):
    return pltpu.make_async_remote_copy(
        src_ref=src,
        dst_ref=dst,
        send_sem=send_sem,
        recv_sem=recv_sem,
        device_id={"band": band, "space": space},
        device_id_type=MESH,
    )


def whole_kernel(
    n_x, n_y, orb, pot, rotation_in, gram, projected, rotated,
    rotation, own_sem, ext, work, pv, edge, rt_all, fb, hb, fr, hr, h_own,
    got, acc, acc_sent, rot, rows, back_out, back_in, part, summed, last, sums, done,
    a_send, a_recv, b_send, b_recv, v_send, v_recv, d_send, d_recv,
    f_send, f_recv, h_send, h_recv, r_send, r_recv,
    right_send, right_recv, left_send, left_recv, core_send, core_recv,
    back_send, back_recv, y_send, y_recv, z_send, z_recv,
):
    bi, si = lax.axis_index("band"), lax.axis_index("space")
    zh, x = bi // n_x, lax.rem(bi, n_x)
    y, q = si // 4, lax.rem(si, 4)
    zl, c = q // 2, lax.rem(q, 2)
    z = zh * 2 + zl
    low, high = y > 0, y < n_y - 1
    right_b = zh * n_x + lax.rem(x + 1, n_x)
    left_b = zh * n_x + lax.rem(x + n_x - 1, n_x)
    mate = y * 4 + (1 - zl) * 2 + c
    core = y * 4 + zl * 2 + (1 - c)

    def along(e):
        other = lax.rem(z * 2 + c + e, 2 * Z)
        oz, oc = other // 2, lax.rem(other, 2)
        return oz, oc, (oz // 2) * n_x + x, y * 4 + lax.rem(oz, 2) * 2 + oc

    def along_z(d):
        other = lax.rem(z + d, Z)
        return other, (other // 2) * n_x + x, y * 4 + lax.rem(other, 2) * 2 + c

    barrier = pltpu.get_barrier_semaphore()

    def greet(band, space):
        pl.semaphore_signal(
            barrier, inc=1, device_id={"band": band, "space": space}, device_id_type=MESH
        )

    for e in range(1, 2 * Z):
        _, _, band, space = along(e)
        greet(band, space)
    for d in range(1, n_y):
        greet(bi, lax.rem(y + d, n_y) * 4 + q)
    greet(right_b, si)
    greet(left_b, si)

    blank = jnp.zeros((PAD, NZ), F32)

    def clear(p, carry):
        for o in range(4):
            ext[o, p, 0:PAD] = blank
            ext[o, p, PAD + NY : TALL] = blank
        for o in range(2):
            work[o, p, 0:PAD] = blank
            work[o, p, PAD + NY : TALL] = blank
        return carry

    lax.fori_loop(0, 24, clear, 0)

    def empty(first, slab, side):
        def body(p, carry):
            for o in range(4):
                ext[o, first + p, DATA] = jnp.zeros((NY, NZ), F32)
            return carry

        lax.fori_loop(0, 8, body, 0)
        pv[slab] = jnp.zeros((2, 2, 2, NY, NZ), F32)
        edge[side] = jnp.zeros((4, NY, NZ), F32)

    @pl.when(y == 0)
    def _():
        empty(0, 0, 0)

    @pl.when(y == n_y - 1)
    def _():
        empty(16, 2, 1)

    pl.semaphore_wait(barrier, 2 * Z - 1 + n_y - 1 + 2)

    v_mate = send(pot, pv.at[1, zl, c], v_send.at[0], v_recv.at[0], bi, mate)
    v_mate.start()

    def partner(d):
        return (1 - zl if d >= 2 else zl) * 2 + (1 - c if d % 2 else c)

    def pair_of(p):
        return slice(2 * p, 2 * p + 2)

    def a_copy(p, d):
        to = partner(d)
        return send(
            orb.at[pl.ds(4 * to + 2 * p, 2)], ext.at[pair_of(p), pl.ds(8 + 2 * q, 2), DATA],
            a_send.at[p, d - 1], a_recv.at[p, d - 1], bi, y * 4 + to,
        )

    def a_wait(p, d):
        of = partner(d)
        send(
            orb.at[pl.ds(4 * q + 2 * p, 2)], ext.at[pair_of(p), pl.ds(8 + 2 * of, 2), DATA],
            a_send.at[p, d - 1], a_recv.at[p, d - 1], bi, y * 4 + of,
        ).wait_recv()

    def own_copy(p):
        return pltpu.make_async_copy(
            orb.at[pl.ds(4 * q + 2 * p, 2)], ext.at[pair_of(p), pl.ds(8 + 2 * q, 2), DATA],
            own_sem.at[p],
        )

    def b_copy(p, d, side):
        of = partner(d)
        here = ext.at[pair_of(p), pl.ds(8 + 2 * of, 2), DATA]
        if d == 0:
            here = orb.at[pl.ds(4 * q + 2 * p, 2)]
        return send(
            here, ext.at[pair_of(p), pl.ds(16 * side + 2 * of, 2), DATA],
            b_send.at[p, d, side], b_recv.at[p, d, side], bi, si + 4 - 8 * side,
        )

    def pass_on(p, d):
        @pl.when(high)
        def _():
            b_copy(p, d, 0).start()

        @pl.when(low)
        def _():
            b_copy(p, d, 1).start()

    for p in range(2):
        for d in (2, 1, 3):
            a_copy(p, d).start()
        if p == 0:
            pass_on(0, 0)
    load_pot = pltpu.make_async_copy(pot, pv.at[1, zl, c], own_sem.at[2])
    load_pot.start()
    load_rotation = pltpu.make_async_copy(rotation_in, rotation, own_sem.at[3])
    load_rotation.start()
    for p in range(2):
        own_copy(p).start()

    v_up = send(pv.at[1, :, c], pv.at[0, :, c], v_send.at[1], v_recv.at[1], bi, si + 4)
    v_down = send(pv.at[1, :, c], pv.at[2, :, c], v_send.at[2], v_recv.at[2], bi, si - 4)

    a_wait(0, 1)
    pass_on(0, 1)
    load_pot.wait()
    v_mate.wait_recv()

    @pl.when(high)
    def _():
        v_up.start()

    @pl.when(low)
    def _():
        v_down.start()

    a_wait(0, 2)
    pass_on(0, 2)
    a_wait(0, 3)
    pass_on(0, 3)
    pass_on(1, 0)
    for d in (1, 2, 3):
        a_wait(1, d)
        pass_on(1, d)
    load_rotation.wait()
    for p in range(2):
        own_copy(p).wait()

    count = rotation.shape[1]
    i = lax.broadcasted_iota(jnp.int32, (count, count), 0)
    k = lax.broadcasted_iota(jnp.int32, (count, count), 1)
    half = n_x * 16
    source = (
        16 * (((k // 4) % 4) * n_x + (k // 16) % n_x)
        + 8 * ((k // 2) % 2)
        + 4 * ((k // half) % 2)
        + 2 * (k // (2 * half))
        + k % 2
    )
    order = jnp.where(i == source, 1.0, 0.0).astype(BF16)
    my_rt = pl.ds(pl.multiple_of(16 * zh, 16), 16)
    rt_all[my_rt] = lax.dot_general(
        rotation[...].astype(BF16), order, (((1,), (0,)), ((), ())), preferred_element_type=F32
    ).astype(BF16)

    def r_copy(d):
        to = lax.rem(zh + d, ZH)
        return send(
            rt_all.at[my_rt], rt_all.at[my_rt],
            r_send.at[d - 1], r_recv.at[d - 1], to * n_x + x, si,
        )

    def r_wait(d):
        of = lax.rem(zh + ZH - d, ZH)
        theirs = rt_all.at[pl.ds(pl.multiple_of(16 * of, 16), 16)]
        send(theirs, theirs, r_send.at[d - 1], r_recv.at[d - 1], of * n_x + x, si).wait_recv()

    for d in range(1, ZH):
        r_copy(d).start()

    @pl.when(low)
    def _():
        v_up.wait_recv()

    @pl.when(high)
    def _():
        v_down.wait_recv()

    v_core = send(pv.at[:, :, c], pv.at[:, :, c], v_send.at[3], v_recv.at[3], bi, core)
    v_core.start()
    send(
        pv.at[:, :, 1 - c], pv.at[:, :, 1 - c], v_send.at[3], v_recv.at[3], bi, core
    ).wait_recv()

    centre, coefficients = steps()
    lane = lax.broadcasted_iota(jnp.int32, (1, NZ), 1)

    def potential(p):
        return pv[p // 8, lax.rem(p, 8) // 4, lax.rem(p, 4) // 2, lax.rem(p, 2)]

    def planes(src, s0, dst, d0, p, width, scale, back, shift):
        old = dst[pl.ds(d0, 2), pl.ds(p, width), DATA] if back != 0.0 else None
        mid = src[pl.ds(s0, 2), pl.ds(p - 1, width + 2), DATA]
        above = src[pl.ds(s0, 2), pl.ds(p, width), PAD - 1 : PAD + NY - 1]
        below = src[pl.ds(s0, 2), pl.ds(p, width), PAD + 1 : PAD + NY + 1]
        for k in range(width):
            now = mid[:, k + 1]
            flat = now.reshape(2 * NY, NZ)
            left = jnp.where(lane == 0, 0.0, pltpu.roll(flat, 1, 1))
            right = jnp.where(lane == NZ - 1, 0.0, pltpu.roll(flat, NZ - 1, 1))
            near = (left + right).reshape(2, NY, NZ)
            near = near + ((above[:, k] + below[:, k]) + (mid[:, k] + mid[:, k + 2]))
            level = (potential(p + k) + shift) * scale
            new = near * (-0.5 * scale) + level[None] * now
            if back != 0.0:
                new = new - back * old[:, k]
            dst[pl.ds(d0, 2), p + k, DATA] = new

    def apply(src, s0, dst, d0, first, count, scale, back, shift):
        def body(i, carry):
            planes(src, s0, dst, d0, first + 4 * i, 4, scale, back, shift)
            return carry

        lax.fori_loop(0, count // 4, body, 0)
        if count % 4:
            planes(src, s0, dst, d0, first + count - 2, 2, scale, back, shift)

    def f_copy(pair, d):
        other, band, space = along_z(d)
        return send(
            fb.at[pair, other], fr.at[z, pair],
            f_send.at[pair, d - 1], f_recv.at[pair, d - 1], band, space,
        )

    def h_copy(pair, d):
        other, band, space = along_z(d)
        return send(
            hb.at[pair, other], hr.at[z, pair],
            h_send.at[pair, d - 1], h_recv.at[pair, d - 1], band, space,
        )

    far = (4, 3, 5, 2, 6, 1, 7)

    def edge_up(pair):
        return send(
            ext.at[pl.ds(2 * pair, 2), 15, DATA], edge.at[0, pl.ds(2 * pair, 2)],
            d_send.at[pair, 0], d_recv.at[pair, 0], bi, si + 4,
        )

    def edge_down(pair):
        return send(
            ext.at[pl.ds(2 * pair, 2), 8, DATA], edge.at[1, pl.ds(2 * pair, 2)],
            d_send.at[pair, 1], d_recv.at[pair, 1], bi, si - 4,
        )

    def filtered(pair):
        for d in range(4):

            @pl.when(low)
            def _():
                b_copy(pair, d, 0).wait_recv()
                b_copy(pair, d, 1).wait_send()

            @pl.when(high)
            def _():
                b_copy(pair, d, 1).wait_recv()
                b_copy(pair, d, 0).wait_send()

        for t, (scale, back) in enumerate(coefficients, 1):
            src, s0, dst, d0 = (ext, 2 * pair, work, 0) if t % 2 else (work, 0, ext, 2 * pair)
            apply(src, s0, dst, d0, t, 24 - 2 * t, scale, back, 3.0 - centre)
            if t < DEGREE:

                @pl.when(y == 0)
                def _():
                    dst[pl.ds(d0, 2), 7, DATA] = jnp.zeros((2, NY, NZ), F32)

                @pl.when(y == n_y - 1)
                def _():
                    dst[pl.ds(d0, 2), 16, DATA] = jnp.zeros((2, NY, NZ), F32)

        def rounded(p, carry):
            value = ext[pl.ds(2 * pair, 2), 8 + p, DATA].reshape(2 * NY, NZ).astype(BF16)
            fb[pair, p] = value
            ext[pl.ds(2 * pair, 2), 8 + p, DATA] = value.astype(F32).reshape(2, NY, NZ)
            return carry

        lax.fori_loop(0, 8, rounded, 0)
        for d in far:
            f_copy(pair, d).start()
        fr[z, pair] = fb[pair, z]

        @pl.when(high)
        def _():
            edge_up(pair).start()

        @pl.when(low)
        def _():
            edge_down(pair).start()

    def turn(src, pair):
        value = src[:, pair].reshape(Z * 2 * NY, NZ).astype(F32).reshape(Z * 2, NY, NZ)
        value = jnp.swapaxes(value, 0, 1).reshape(NY * Z * 2, NZ).astype(BF16)
        return value.reshape(NY, Z * 2, NZ)

    def block(cls, owner, piece):
        pair, first, size = PIECES[piece]
        return got.at[cls, owner, pair, pl.ds(first, size)]

    def go_right(hop, piece):
        owner = lax.rem(x - hop + n_x, n_x)
        return send(
            block(c, owner, piece), block(c, owner, piece),
            right_send.at[hop, piece], right_recv.at[hop, piece], right_b, si,
        )

    def from_left(hop, piece):
        owner = lax.rem(x - hop - 1 + n_x, n_x)
        return send(
            block(c, owner, piece), block(c, owner, piece),
            right_send.at[hop, piece], right_recv.at[hop, piece], right_b, si,
        )

    def go_left(hop, piece):
        owner = lax.rem(x + hop, n_x)
        return send(
            block(c, owner, piece), block(c, owner, piece),
            left_send.at[hop, piece], left_recv.at[hop, piece], left_b, si,
        )

    def from_right(hop, piece):
        owner = lax.rem(x + hop + 1, n_x)
        return send(
            block(c, owner, piece), block(c, owner, piece),
            left_send.at[hop, piece], left_recv.at[hop, piece], left_b, si,
        )

    def go_core(slot, piece):
        owner = lax.rem(x - slot + n_x, n_x)
        return send(
            block(c, owner, piece), block(c, owner, piece),
            core_send.at[slot, piece], core_recv.at[slot, piece], bi, core,
        )

    def from_core(slot, piece):
        owner = lax.rem(x - slot + n_x, n_x)
        return send(
            block(1 - c, owner, piece), block(1 - c, owner, piece),
            core_send.at[slot, piece], core_recv.at[slot, piece], bi, core,
        )

    def launch(pair):
        for d in range(1, Z):
            f_copy(pair, d).wait_recv()
        got[c, x, pair] = turn(fr, pair)
        n_right, n_left = hops(n_x, pair)
        mine = [k for k in range(len(PIECES)) if PIECES[k][0] == pair]
        for piece in mine:
            if n_right > 0:
                go_right(0, piece).start()
            if n_left > 0:
                go_left(0, piece).start()
        for piece in mine:
            go_core(0, piece).start()

    def serve(hop, piece):
        n_right, n_left = hops(n_x, PIECES[piece][0])
        if hop <= n_right:
            from_left(hop - 1, piece).wait_recv()
            if hop < n_right:
                go_right(hop, piece).start()
            go_core(hop, piece).start()
        if hop <= n_left:
            from_right(hop - 1, piece).wait_recv()
            if hop < n_left:
                go_left(hop, piece).start()
            go_core(n_x - hop, piece).start()

    def applied(pair):
        @pl.when(low)
        def _():
            edge_up(pair).wait_recv()

        @pl.when(high)
        def _():
            edge_down(pair).wait_recv()

        ext[pl.ds(2 * pair, 2), 7, DATA] = edge[0, pl.ds(2 * pair, 2)]
        ext[pl.ds(2 * pair, 2), 16, DATA] = edge[1, pl.ds(2 * pair, 2)]
        apply(ext, 2 * pair, work, 0, 8, 8, 1.0, 0.0, 3.0)

        def stored(p, carry):
            hb[pair, p] = work[:, 8 + p, DATA].reshape(2 * NY, NZ).astype(BF16)
            return carry

        lax.fori_loop(0, 8, stored, 0)
        for d in far:
            h_copy(pair, d).start()
        hr[z, pair] = hb[pair, z]

    def take_applied(pair):
        for d in range(1, Z):
            h_copy(pair, d).wait_recv()
        h_own[pair] = turn(hr, pair)

    def take_core(piece):
        for slot in range(n_x):
            from_core(slot, piece).wait_recv()

    zero = jnp.zeros((4 * 16, NZ), BF16)

    def correlate(piece):
        pair, first, size = PIECES[piece]

        def body(g, carry):
            total = None
            for k in range(ROWS):
                r = first + g * ROWS + k
                ours = jnp.concatenate(
                    [got[c, x, 0, r], got[c, x, 1, r], h_own[0, r], h_own[1, r]], axis=0
                )
                factor = jnp.concatenate(
                    [
                        jnp.concatenate([ours, zero], axis=0),
                        jnp.concatenate([zero, ours], axis=0),
                    ],
                    axis=1,
                )
                both = jnp.concatenate(
                    [got[cls, :, pair, r].reshape(n_x * 16, NZ) for cls in range(2)], axis=1
                )
                value = lax.dot_general(
                    both, factor, (((1,), (1,)), ((), ())), preferred_element_type=F32
                )
                total = value if total is None else total + value
            acc[pair] += total.reshape(n_x, 16, NZ)
            return carry

        lax.fori_loop(0, size // ROWS, body, 0)

    my_rows = pl.ds(pl.multiple_of(32 * c, 32), 32)

    def rotate(piece):
        pair, first, size = PIECES[piece]

        ours = rt_all[my_rows, pair * 2 * half : (pair + 1) * 2 * half]

        def body(g, carry):
            for k in range(ROWS):
                r = first + g * ROWS + k
                every = got[:, :, pair, r].reshape(2 * n_x * 16, NZ)
                value = jnp.dot(ours, every, preferred_element_type=F32)
                if pair == 0:
                    rot[r] = value
                else:
                    rows[k] = rot[r] + value
            return carry

        lax.fori_loop(0, size // ROWS, body, 0)

    home_q = z // 2

    def is_self(m):
        return (home_q == q) & (2 * c + m == zh)

    def give_back(m, chunk):
        return send(
            back_out.at[chunk, m], back_in.at[lax.rem(z, 2), chunk],
            back_send.at[m, chunk], back_recv.at[lax.rem(z, 2), chunk],
            (2 * c + m) * n_x + x, y * 4 + home_q,
        )

    def come_back(plane, chunk):
        return send(
            back_out.at[chunk, 0], back_in.at[plane, chunk],
            back_send.at[0, chunk], back_recv.at[plane, chunk], bi, core,
        )

    def return_rows(chunk):
        value = jnp.swapaxes(rows[...], 0, 1).reshape(2, 16 * ROWS, NZ).astype(BF16)
        back_out[chunk] = value
        for m in range(2):

            @pl.when(is_self(m))
            def _():
                back_in[lax.rem(z, 2), chunk] = back_out[chunk, m]

            @pl.when(jnp.logical_not(is_self(m)))
            def _():
                give_back(m, chunk).start()

    def y_copy(pair, d):
        to = lax.rem(y + d, n_y)
        return send(
            acc_sent.at[pair, to], part.at[pair, y],
            y_send.at[pair, d - 1], y_recv.at[pair, d - 1], bi, to * 4 + q,
        )

    def y_begin(pair):
        for to in range(n_y):
            for k in range(4):
                zh_i, x_i = (4 * to + k) // n_x, (4 * to + k) % n_x
                acc_sent[pair, to, 4 * k : 4 * k + 4] = acc[pair, x_i, 4 * zh_i : 4 * zh_i + 4]
        for d in sorted(range(1, n_y), key=lambda d: -min(d, n_y - d)):
            y_copy(pair, d).start()
        part[pair, y] = acc_sent[pair, y]

    acc[...] = jnp.zeros_like(acc)
    pieces = len(PIECES)
    filtered(0)
    filtered(1)
    launch(0)

    def serve_pair(hop, pair):
        for piece in range(CHUNKS * pair, CHUNKS * (pair + 1)):
            serve(hop, piece)

    applied(0)
    serve_pair(1, 0)
    launch(1)
    applied(1)
    serve_pair(2, 0)
    serve_pair(1, 1)
    take_applied(0)
    serve_pair(3, 0)
    serve_pair(2, 1)
    take_applied(1)
    for d in range(1, ZH):
        r_wait(d)
    serve_pair(4, 0)
    serve_pair(3, 1)
    for piece in range(CHUNKS):
        take_core(piece)
        rotate(piece)
        correlate(piece)
    serve_pair(4, 1)
    y_begin(0)
    for piece in range(CHUNKS, pieces):
        take_core(piece)
        if piece == pieces - 1:
            break
        rotate(piece)
        return_rows(piece - CHUNKS)
        correlate(piece)
    correlate(pieces - 1)

    y_begin(1)
    rotate(pieces - 1)
    return_rows(CHUNKS - 1)
    for pair in range(2):
        for d in range(1, n_y):
            y_copy(pair, d).wait_recv()
        total = part[pair, 0]
        for k in range(1, n_y):
            total = total + part[pair, k]
        for k in range(4):
            summed[k // 2, k % 2, 4 * pair : 4 * pair + 4] = total[4 * k : 4 * k + 4]

    def z_copy(d):
        oz, band, space = along_z(d)
        return send(
            summed.at[lax.rem(oz, 2)], last.at[z],
            z_send.at[d - 1], z_recv.at[d - 1], band, space,
        )

    for d in far:
        z_copy(d).start()
    last[z] = summed[zl]

    for chunk in range(CHUNKS):
        for plane in range(2):
            from_me = (2 * q + plane == z) & (c == zh // 2)

            @pl.when(jnp.logical_not(from_me))
            def _():
                come_back(plane, chunk).wait_recv()

            rotated[:, plane, chunk * ROWS : (chunk + 1) * ROWS] = (
                back_in[plane, chunk].astype(F32).reshape(16, ROWS, NZ)
            )

    for d in range(1, Z):
        z_copy(d).wait_recv()
    value = last[0]
    for k in range(1, Z):
        value = value + last[k]
    sums[0] = value
    done[c] = sums[0, c]
    trade = send(
        sums.at[0, 1 - c], done.at[c], v_send.at[4], v_recv.at[4], bi, core
    )
    trade.start()
    send(
        sums.at[0, c], done.at[1 - c], v_send.at[4], v_recv.at[4], bi, core
    ).wait_recv()
    n = lax.broadcasted_iota(jnp.int32, (64, NZ), 0)
    l = lax.broadcasted_iota(jnp.int32, (64, NZ), 1)
    lane_of = (
        64 * ((n // 16) % 2) + 32 * (n // 32)
        + 16 * ((n // 2) % 2) + 4 * zh + 2 * ((n // 8) % 2) + n % 2
    )
    picked = None
    for cls in range(2):
        value = done[cls]
        select = jnp.where((l == lane_of) & ((n // 4) % 2 == cls), 1.0, 0.0)
        value = lax.dot_general(
            select, value, (((1,), (1,)), ((), ())),
            precision=lax.Precision.HIGHEST, preferred_element_type=F32,
        )
        picked = value if picked is None else picked + value
    r = lax.broadcasted_iota(jnp.int32, (8, 16), 0)
    i = lax.broadcasted_iota(jnp.int32, (8, 16), 1)
    for side, out in enumerate((gram, projected)):
        value = None
        for cls in range(2):
            select = jnp.where(
                i == 8 * ((r // 2) % 2) + 4 * cls + 2 * (r // 4) + r % 2, 1.0, 0.0
            )
            first = 32 * side + 16 * cls
            term = jnp.dot(
                picked[first : first + 16], select,
                precision=lax.Precision.HIGHEST, preferred_element_type=F32,
            )
            value = term if value is None else value + term
        out[...] = value

    for d in range(1, ZH):
        r_copy(d).wait_send()
    for p in range(2):
        for d in range(1, 4):
            a_copy(p, d).wait_send()
    v_mate.wait_send()
    v_core.wait_send()
    for pair in range(2):
        for d in range(1, Z):
            f_copy(pair, d).wait_send()
            h_copy(pair, d).wait_send()

    @pl.when(high)
    def _():
        v_up.wait_send()
        for pair in range(2):
            edge_up(pair).wait_send()

    @pl.when(low)
    def _():
        v_down.wait_send()
        for pair in range(2):
            edge_down(pair).wait_send()

    for piece in range(pieces):
        n_right, n_left = hops(n_x, PIECES[piece][0])
        for hop in range(n_right):
            go_right(hop, piece).wait_send()
        for hop in range(n_left):
            go_left(hop, piece).wait_send()
        for slot in range(n_x):
            go_core(slot, piece).wait_send()
    for chunk in range(CHUNKS):
        for m in range(2):

            @pl.when(jnp.logical_not(is_self(m)))
            def _():
                give_back(m, chunk).wait_send()

    for pair in range(2):
        for d in range(1, n_y):
            y_copy(pair, d).wait_send()
    for d in range(1, Z):
        z_copy(d).wait_send()
    trade.wait_send()


def shards(orbitals, potential, rotation):
    n_x = lax.axis_size("band") // ZH
    n_y = lax.axis_size("space") // 4
    top, pieces = max(n_x // 2, 1), len(PIECES)
    dma = pltpu.SemaphoreType.DMA

    def kernel(*refs):
        whole_kernel(n_x, n_y, *refs)

    return pl.pallas_call(
        kernel,
        out_shape=(
            VMEM((16, 16), F32),
            VMEM((16, 16), F32),
            VMEM(orbitals.shape, F32),
        ),
        in_specs=[pl.BlockSpec(memory_space=pltpu.HBM)] * 3,
        out_specs=[pl.BlockSpec(memory_space=VMEM)] * 3,
        scratch_shapes=[
            VMEM(rotation.shape[::-1], F32), dma((4,)),
            VMEM((4, 24, TALL, NZ), F32),
            VMEM((2, 24, TALL, NZ), F32),
            VMEM((3, 2, 2, 2, NY, NZ), F32),
            VMEM((2, 4, NY, NZ), F32),
            VMEM((16 * ZH, rotation.shape[0]), BF16),
            VMEM((2, Z, 2 * NY, NZ), BF16),
            VMEM((2, Z, 2 * NY, NZ), BF16),
            VMEM((Z, 2, 2 * NY, NZ), BF16),
            VMEM((Z, 2, 2 * NY, NZ), BF16),
            VMEM((2, NY, 2 * Z, NZ), BF16),
            VMEM((2, n_x, 2, NY, 2 * Z, NZ), BF16),
            VMEM((2, n_x, 2 * Z, NZ), F32),
            VMEM((2, n_y, 16, NZ), F32),
            VMEM((NY, 32, NZ), F32),
            VMEM((ROWS, 32, NZ), F32),
            VMEM((CHUNKS, 2, 16 * ROWS, NZ), BF16),
            VMEM((2, CHUNKS, 16 * ROWS, NZ), BF16),
            VMEM((2, n_y, 16, NZ), F32),
            VMEM((2, 2, 8, NZ), F32),
            VMEM((Z, 2, 8, NZ), F32),
            VMEM((1, 2, 8, NZ), F32),
            VMEM((2, 8, NZ), F32),
            dma((2, 3)), dma((2, 3)), dma((2, 4, 2)), dma((2, 4, 2)), dma((5,)), dma((5,)),
            dma((2, 2)), dma((2, 2)), dma((2, Z - 1)), dma((2, Z - 1)),
            dma((2, Z - 1)), dma((2, Z - 1)), dma((ZH - 1,)), dma((ZH - 1,)),
            dma((top, pieces)), dma((top, pieces)), dma((top, pieces)), dma((top, pieces)),
            dma((n_x, pieces)), dma((n_x, pieces)), dma((2, CHUNKS)), dma((2, CHUNKS)),
            dma((2, n_y - 1)), dma((2, n_y - 1)), dma((Z - 1,)), dma((Z - 1,)),
        ],
        compiler_params=pltpu.CompilerParams(
            collective_id=0, has_side_effects=True, vmem_limit_bytes=60 * 2**20
        ),
    )(orbitals, potential, rotation.T)


def solution(mesh):
    placed = (P("band", "space", None, None), P("space", None, None), P(None, "band"))
    return jax.shard_map(
        shards,
        mesh=mesh,
        in_specs=placed,
        out_specs=(P("band", "space"), P("band", "space"), P("band", "space", None, None)),
        check_vma=False,
    )
```
